1024 devices in a mesh: section: 2 (over core), dp: 16 (over x, y), expert: 32 (over z).
Axes of the slice: x: 4, y: 4, z: 32, core: 2. Of those that a mesh axis runs over, the one named last changes fastest.
Arguments:
- tokens: bfloat16 [16384, 5120], P(('section', 'expert'), 'dp'), may hold values from -6 to 6
- routes: int32 [16384, 4], P(('section', 'expert')), may hold values from 0 to 127, all different within a row; in each aligned block of 256 rows (0 to 255, 256 to 511, ...) at most 10 rows name the same one
- route_weights: float32 [16384, 4], P(('section', 'expert')), may hold values from 0.05 to 0.6
- w_gate_up: bfloat16 [128, 5120, 1536], P(('section', 'expert'), 'dp'), may hold values from -0.078125 to 0.078125
- w_down: bfloat16 [128, 768, 5120], P(('section', 'expert'), None, 'dp'), may hold values from -0.21875 to 0.21875
- w_latent: bfloat16 [5120, 512], P('dp'), may hold values from -0.078125 to 0.078125
- latent_gain: float32 [512], replicated, may hold values from 0.5 to 1.5
- lengths: int32 [64, 16], P(('section', 'expert')), may hold values from 1 to 32, 256 in all within a row
- placement: int32 [64, 16], P(('section', 'expert')), may hold values from 0 to 15, each once within a row
Outputs:
- mixed_out: bfloat16 [16384, 5120], P(('section', 'expert'), 'dp')
- latent_cache: bfloat16 [16, 64, 32, 512], P('dp', ('section', 'expert'))
The draws below stay inside these ranges and needn't reach their ends.
Inputs may be any that keep to these rules, and one draw needn't show every extreme that they name: `routes`: in each aligned block of 256 rows (the rows of one row group) no expert is named more than 10 times, a bound that some block reaches. `lengths`: each row sums to 256 and its largest entry is exactly 32. `placement`: each row holds every number of 0 to 15 once.
All inputs are finite; a program needn't handle non-finite values.
Results may differ from the reference program's by a relative error of at most 0.029.
Values may be sent and summed in bfloat16 or wider, within the bound.
No kernel may reach another device: no remote copies, remote signals or barrier semaphores. Data moves between devices by JAX's collectives and lax.ppermute only.
A program may use at most 32 MiB of HBM per device.

```python
import math
import jax
import jax.numpy as jnp
import numpy as np
from jax import lax

D = 5120
FF = 768
LAT = 512
TOK_DEV = 256
TOP = 4
GROUPS = 64
EXPERTS = 128
TOKENS = 16384
CAP = 10
INST = 16
MOST = 32
N_DP = 16


def level_of(stream_key, shape, shards, low, high):
    level = 1.0
    for axis_at, shards_of in shards:
        draws = jax.random.uniform(jax.random.fold_in(jax.random.fold_in(stream_key, 6), axis_at), (shards_of,), jnp.float32, low / len(shards), high / len(shards))
        level = level * jnp.repeat(jnp.exp(draws), shape[axis_at] // shards_of).reshape((-1,) + (1,) * (len(shape) - 1 - axis_at))
    return level


def profile(number_of, total, most, skew):
    loads = [(1 << 20) // math.isqrt(rank ** skew) + 1 for rank in range(2, number_of + 1)]
    surplus, given = total - most - (number_of - 1), [1] * (number_of - 1)
    while surplus > 0:
        movable = [i for i in range(number_of - 1) if given[i] < most]
        pool, budget = sum([loads[i] for i in movable]), surplus
        for i in movable:
            extra = min(most - given[i], max(1, budget * loads[i] // pool), surplus)
            given[i] = given[i] + extra
            surplus = surplus - extra
    return np.array([most] + given)


def ragged(own_key, count, total, limit, slope):
    if count == 2:
        one = jax.random.randint(own_key, (), max(1, total - limit), min(limit, total - 1) + 1)
        return jnp.stack([one, total - one])
    sizes = jnp.asarray(profile(count, total, limit, slope), jnp.int32)
    couples = (count - 1) // 2
    source_of, sink = sizes[1:1 + 2 * couples:2], sizes[2:2 + 2 * couples:2]
    room = jnp.minimum(source_of - 1, limit - sink)
    passed = jax.random.randint(jax.random.fold_in(own_key, 1), (couples,), 0, 1 << 20) % (room + 1)
    sizes = sizes.at[1:1 + 2 * couples:2].set(source_of - passed).at[2:2 + 2 * couples:2].set(sink + passed)
    return sizes[jax.random.permutation(jax.random.fold_in(own_key, 2), count)]


def routed_block(key, own, number, rows, number_of, top, bound, lean):
    ranking = jax.random.permutation(key, number_of)
    crowded, usual = portions_of(number_of, rows * top, bound, lean, True), portions_of(number_of, rows * top, bound, lean, False)
    places = jnp.arange(number_of)

    def named(sizes, turn):
        used = int((sizes > 0).sum())
        fixed = max(1, used // 4)
        passed = fixed + (places - fixed + turn * (used - fixed)) % max(1, number_of - fixed)
        return jnp.zeros((number_of,), jnp.int32).at[ranking[jnp.where(places < fixed, places, passed)]].set(jnp.asarray(sizes, jnp.int32))

    sizes = jnp.where(number % 4 == 0, named(crowded, number // 4), named(usual, number - number // 4 - 1))
    mixed = jax.random.permutation(jax.random.fold_in(own, 3), number_of)
    source_of, taker = mixed[0:number_of // 2 * 2:2], mixed[1:number_of // 2 * 2:2]
    slack = jnp.minimum(sizes[source_of] - 1, bound - sizes[taker]) // 2
    slack = jnp.where((source_of == ranking[0]) | (taker == ranking[0]) | (sizes[taker] == 0), 0, jnp.maximum(slack, 0))
    passed = jax.random.randint(jax.random.fold_in(own, 4), (number_of // 2,), 0, 1 << 20) % (slack + 1)
    sizes = sizes.at[source_of].add(-passed).at[taker].add(passed)
    members = jnp.searchsorted(jnp.cumsum(sizes), jnp.arange(rows * top), side="right").astype(jnp.int32)
    table = members.reshape(top, rows).T
    table = table[jax.random.permutation(jax.random.fold_in(own, 1), rows)]
    turn = jax.random.randint(jax.random.fold_in(own, 2), (rows, 1), 0, top)
    return jnp.take_along_axis(table, (jnp.arange(top)[None, :] + turn) % top, axis=1)


def portions_of(number_of, total, bound, lean, full):
    weights = [(1 << 20) // math.isqrt(standing ** lean) + 1 for standing in range(1, number_of + 1)]
    largest = bound if full else min(bound, max(-(-total // number_of), total * weights[0] // sum(weights)))
    least = 1 if total - largest >= number_of - 1 else 0
    holding, surplus = [largest] + [least] * (number_of - 1), total - largest - least * (number_of - 1)
    while surplus > 0:
        free = [i for i in range(1, number_of) if holding[i] < largest] or [i for i in range(1, number_of) if holding[i] < bound]
        pool, left = sum([weights[i] for i in free]), surplus
        for i in free:
            addition = min(bound - holding[i], max(1, left * weights[i] // pool), surplus)
            holding[i] = holding[i] + addition
            surplus = surplus - addition
    return np.array(holding)


def scatter_about(own_key, dims, scale, limit, pieces=(), kind=jnp.bfloat16):
    values = jax.random.normal(own_key, dims, jnp.float32) * scale
    if len(pieces) > 0:
        values = level_of(own_key, dims, pieces, -0.22, 0.18) * values
    return jnp.clip(values, min=-limit, max=limit).astype(kind)


def setup_inputs(seed: int = 0) -> dict:
    streams_of = jax.random.split(jax.random.key(seed), 10)
    tokens = scatter_about(streams_of[0], (TOKENS, D), 1.0, 6.0, ((0, 64), (1, 16)))
    routes_keys = jax.random.split(jax.random.fold_in(streams_of[1], 1), TOKENS // TOK_DEV)
    routes_turns = jax.random.permutation(jax.random.fold_in(streams_of[1], 3), TOKENS // TOK_DEV)
    routes = jax.vmap(lambda own, number: routed_block(jax.random.fold_in(streams_of[1], 2), own, number, TOK_DEV, EXPERTS, TOP, CAP, 2))(routes_keys, routes_turns).reshape((TOKENS, TOP))
    route_weights = jnp.clip(0.05 + 0.55 * jax.random.uniform(streams_of[2], (TOKENS, TOP), jnp.float32) ** level_of(streams_of[2], (TOKENS, TOP), ((0, 64),), -0.2, 0.2), 0.05, 0.6)
    w_gate_up = scatter_about(streams_of[3], (EXPERTS, D, 2 * FF), D ** -0.5, 0.078125, ((0, 64), (1, 16)))
    w_down = scatter_about(streams_of[4], (EXPERTS, FF, D), FF ** -0.5, 0.21875, ((0, 64), (2, 16)))
    w_latent = scatter_about(streams_of[5], (D, LAT), D ** -0.5, 0.078125, ((0, 16),))
    latent_gain = jnp.clip(1.0 + 0.1 * jax.random.normal(streams_of[6], (LAT,), jnp.float32), 0.5, 1.5)
    lengths = jax.vmap(lambda own: ragged(own, INST, TOK_DEV, MOST, 2))(jax.random.split(streams_of[7], GROUPS)).reshape((GROUPS, INST)).astype(jnp.int32)
    placement = jax.vmap(lambda own: jax.random.permutation(own, INST))(jax.random.split(streams_of[8], GROUPS)).reshape((GROUPS, INST)).astype(jnp.int32)
    return dict(tokens=tokens, routes=routes, route_weights=route_weights, w_gate_up=w_gate_up, w_down=w_down, w_latent=w_latent, latent_gain=latent_gain, lengths=lengths, placement=placement)


def slot_table(routes):
    route_ids = routes.reshape(GROUPS, TOK_DEV * TOP)
    one_hot = (route_ids[:, :, None] == jnp.arange(EXPERTS, dtype=jnp.int32)[None, None, :]).astype(jnp.int32)
    earlier = jnp.cumsum(one_hot, axis=1) - one_hot
    slot_rank = lax.optimization_barrier(jnp.sum(earlier * one_hot, axis=2))
    sources = jnp.arange(GROUPS, dtype=jnp.int32)[:, None]
    flat_index = (route_ids * GROUPS + sources) * CAP + slot_rank
    return flat_index.reshape(-1)

def blockwise_sum(partial_terms):
    rounded = lax.optimization_barrier(partial_terms.astype(jnp.bfloat16))
    return lax.optimization_barrier(jnp.sum(rounded.astype(jnp.float32), axis=1))

def reference(tokens, routes, route_weights, w_gate_up, w_down, w_latent, latent_gain, lengths, placement):
    blocks = N_DP
    width_share = D // blocks
    flat_index = slot_table(routes)
    token_index = jnp.arange(TOKENS * TOP, dtype=jnp.int32) // TOP
    row_table = jnp.full((EXPERTS * GROUPS * CAP,), TOKENS, jnp.int32).at[flat_index].set(token_index)
    row_table = row_table.reshape(EXPERTS, GROUPS * CAP)
    padded_tokens = jnp.concatenate([tokens, jnp.zeros((1, D), tokens.dtype)], axis=0)

    def expert_rows(inputs):
        rows_index, gate_up, down_part = inputs
        row_block = padded_tokens[rows_index].reshape(-1, blocks, width_share).astype(jnp.float32)
        weights = gate_up.reshape(blocks, width_share, 2 * FF).astype(jnp.float32)
        summed = blockwise_sum(jnp.einsum('rgd,gdf->rgf', row_block, weights))
        hidden = (jax.nn.silu(summed[:, :FF]) * summed[:, FF:]).astype(jnp.bfloat16)
        return jnp.dot(hidden, down_part, preferred_element_type=jnp.float32).astype(jnp.bfloat16)
    outputs = lax.map(expert_rows, (row_table, w_gate_up, w_down))
    per_route = outputs.reshape(-1, D)[flat_index].reshape(TOKENS, TOP, D)
    mixed_out = lax.optimization_barrier(jnp.sum(route_weights[:, :, None] * per_route.astype(jnp.float32), axis=1)).astype(jnp.bfloat16)
    token_blocks = tokens.reshape(TOKENS, blocks, width_share).astype(jnp.float32)
    latent_weights = w_latent.reshape(blocks, width_share, LAT).astype(jnp.float32)
    latent = blockwise_sum(jnp.einsum('tgd,gdl->tgl', token_blocks, latent_weights))
    offsets = jnp.cumsum(lengths, axis=1) - lengths
    starts = jnp.take_along_axis(offsets, placement, axis=1)
    span_list = jnp.take_along_axis(lengths, placement, axis=1)
    positions = jnp.arange(MOST, dtype=jnp.int32)
    columns = jnp.arange(GROUPS, dtype=jnp.int32)[:, None, None] * TOK_DEV
    row_index = columns + starts[:, :, None] + positions[None, None, :]
    live_rows = positions[None, None, :] < span_list[:, :, None]
    picked = latent[jnp.clip(row_index, 0, TOKENS - 1)]
    inverse_rms = lax.rsqrt(lax.optimization_barrier(jnp.mean(picked * picked, axis=-1, keepdims=True)) + 1e-06)
    latent_cache = jnp.where(live_rows[..., None], picked * inverse_rms * latent_gain, 0.0).astype(jnp.bfloat16)
    latent_cache = jnp.transpose(latent_cache, (1, 0, 2, 3))
    return (mixed_out, latent_cache)
```

```python
import functools

import jax
import jax.numpy as jnp
from jax import lax
from jax.experimental import pallas as pl
from jax.experimental.pallas import tpu as pltpu
from jax.sharding import PartitionSpec as P

SE = ("section", "expert")
NT = (((1,), (1,)), ((), ()))
TN = (((0,), (0,)), ((), ()))
BF = jnp.bfloat16
F32 = jnp.float32


def call(kernel, out_shape, *args, in_specs=None, scratch=(), flops=0, moved=0):
    kwargs = {}
    if in_specs is not None:
        kwargs["in_specs"] = in_specs
        kwargs["grid"] = (1,)
    return pl.pallas_call(
        kernel,
        out_shape=out_shape,
        scratch_shapes=list(scratch),
        cost_estimate=pl.CostEstimate(flops=flops, bytes_accessed=moved, transcendentals=0),
        compiler_params=pltpu.CompilerParams(vmem_limit_bytes=24 * 1024 * 1024),
        **kwargs,
    )(*args)


def iota(shape, dim):
    return lax.broadcasted_iota(jnp.int32, shape, dim)


def named_and_rank(routes_t, experts):
    tops, rows = routes_t.shape
    ids = iota((experts, rows), 0)
    named = jnp.zeros((experts, rows), F32)
    for k in range(tops):
        named = named + jnp.where(routes_t[k : k + 1, :] == ids, 1.0, 0.0)
    earlier = (iota((rows, rows), 0) < iota((rows, rows), 1)).astype(F32).astype(BF)
    rank = jnp.dot(named.astype(BF), earlier, preferred_element_type=F32)
    return named, rank


def spread(experts, resident):
    row, col = iota((experts, experts), 0), iota((experts, experts), 1)
    return (col == row - (row & 1) + resident).astype(F32).astype(BF)


def slot_masks(named, rank, resident, lanes):
    experts, rows = named.shape
    pick = spread(experts, resident)
    named_s = jnp.dot(pick, named.astype(BF), preferred_element_type=F32)
    rank_s = jnp.dot(pick, rank.astype(BF), preferred_element_type=F32)
    base = ((iota((experts, rows), 0) & 1) * lanes).astype(F32)
    return [(named_s > 0.5) & (rank_s == base + float(i)) for i in range(lanes)]


def dispatch_kernel(residents, lanes, routes_ref, tokens_ref, out):
    width = tokens_ref.shape[0]
    named, rank = named_and_rank(routes_ref[...], out.shape[0])
    for r in range(residents):
        for i, mask in enumerate(slot_masks(named, rank, r, lanes)):
            rows = lax.dot_general(
                mask.astype(F32).astype(BF), tokens_ref[...], NT, preferred_element_type=F32
            )
            at = (r * lanes + i) * width
            out[:, at : at + width] = rows.astype(BF)


def weights_kernel(residents, lanes, routes_ref, weights_ref, high_ref, low_ref):
    experts = high_ref.shape[1]
    routes_t, weights_t = routes_ref[...], weights_ref[...]
    named, rank = named_and_rank(routes_t, experts)
    ids = iota(named.shape, 0)
    gates = jnp.zeros(named.shape, F32)
    for k in range(routes_t.shape[0]):
        gates = gates + jnp.where(routes_t[k : k + 1, :] == ids, weights_t[k : k + 1, :], 0.0)
    high = gates.astype(BF)
    low = (gates - high.astype(F32)).astype(BF)
    for r in range(residents):
        pick = spread(experts, r)
        high_s = jnp.dot(pick, high, preferred_element_type=F32)
        low_s = jnp.dot(pick, low, preferred_element_type=F32)
        for i, mask in enumerate(slot_masks(named, rank, r, lanes)):
            high_ref[r * lanes + i] = jnp.where(mask, high_s, 0.0).astype(BF)
            low_ref[r * lanes + i] = jnp.where(mask, low_s, 0.0).astype(BF)


def up_kernel(lanes, rows_ref, weight_ref, out, packed):
    slots = rows_ref.shape[0]
    residents, width, columns = weight_ref.shape
    each = lanes * slots
    step = 512 if columns % 512 == 0 else columns
    for r in range(residents):
        for i in range(lanes):
            at = (r * lanes + i) * width
            packed[i * slots : (i + 1) * slots, :] = rows_ref[:, at : at + width]
        for c in range(0, columns, step):
            part = jnp.dot(
                packed[...], weight_ref[r, :, c : c + step], preferred_element_type=F32
            )
            out[r * each : (r + 1) * each, c : c + step] = part.astype(BF)


def hidden_kernel(parts_ref, out):
    blocks = parts_ref.shape[0]
    half = out.shape[2]
    total = parts_ref[0].astype(F32)
    for b in range(1, blocks):
        total = total + parts_ref[b].astype(F32)
    gate, up = total[:, :half], total[:, half:]
    hidden = (gate / (1.0 + jnp.exp(-gate)) * up).astype(BF)
    for b in range(blocks):
        out[b] = hidden


def down_kernel(lanes, hidden_ref, weight_ref, out):
    slots = out.shape[0]
    residents, width, _ = weight_ref.shape
    each = lanes * slots
    for r in range(residents):
        part = lax.dot_general(
            hidden_ref[r * each : (r + 1) * each, :],
            weight_ref[r],
            NT,
            preferred_element_type=F32,
        ).astype(BF)
        for i in range(lanes):
            at = (r * lanes + i) * width
            out[:, at : at + width] = part[i * slots : (i + 1) * slots, :]


def mix_kernel(back_ref, high_ref, low_ref, out):
    width = out.shape[0]
    total = jnp.zeros(out.shape, F32)
    for i in range(high_ref.shape[0]):
        rows = back_ref[:, i * width : (i + 1) * width]
        total = total + lax.dot_general(rows, high_ref[i], TN, preferred_element_type=F32)
        total = total + lax.dot_general(rows, low_ref[i], TN, preferred_element_type=F32)
    out[...] = total.astype(BF)


def latent_kernel(longest, lengths_ref, placement_ref, tokens_ref, weight_ref, out, select, offset):
    requests = lengths_ref.shape[1]
    rows = tokens_ref.shape[1]
    partial = lax.dot_general(tokens_ref[...], weight_ref[...], TN, preferred_element_type=F32)
    run = jnp.int32(0)
    for j in range(requests):
        offset[j] = run
        run = run + lengths_ref[0, j]
    place, position = iota((longest, rows), 0), iota((longest, rows), 1)
    for q in range(requests):
        request = placement_ref[0, q]
        hit = (position == place + offset[request]) & (place < lengths_ref[0, request])
        select[q * longest : (q + 1) * longest, :] = hit.astype(F32).astype(BF)
    picked = jnp.dot(select[...], partial.astype(BF), preferred_element_type=F32)
    out[...] = picked.astype(BF)


def norm_kernel(sum_ref, gain_ref, out):
    total = sum_ref[...].astype(F32)
    scale = lax.rsqrt(jnp.mean(total * total, axis=1, keepdims=True) + 1e-06)
    out[...] = (total * scale * gain_ref[...]).astype(BF)


def exchange(x, axes):
    return lax.all_to_all(x, axes, split_axis=0, concat_axis=0, tiled=True)


def body(
    tokens, routes, route_weights, w_gate_up, w_down, w_latent, latent_gain, lengths, placement
):
    groups = lax.axis_size(SE)
    blocks = lax.axis_size("dp")
    rows, width = tokens.shape
    tops = routes.shape[1]
    residents = w_gate_up.shape[0]
    hidden_units = w_down.shape[1]
    latent_width = w_latent.shape[1]
    experts = residents * groups
    capacity = 5 * rows * tops // (4 * experts)
    lanes = capacity // 2
    slots = 2 * groups
    longest = 2 * rows // blocks
    total_slots = experts * capacity
    share = total_slots // blocks
    row = residents * lanes * width
    shape = jax.ShapeDtypeStruct
    tokens_t, routes_t, gates_t = tokens.T, routes.T, route_weights.T
    down_t = w_down.transpose(0, 2, 1)
    vmem = pl.BlockSpec(memory_space=pltpu.VMEM)
    smem = pl.BlockSpec(memory_space=pltpu.SMEM)

    with jax.named_scope("dispatch"):
        outgoing = call(
            functools.partial(dispatch_kernel, residents, lanes),
            shape((slots, row), BF),
            routes_t,
            tokens_t,
            flops=2 * rows * width * total_slots,
            moved=2 * total_slots * width,
        )
        arrived = exchange(outgoing.reshape(groups, 2, row), SE).reshape(slots, row)

    with jax.named_scope("latent"):
        picked = call(
            functools.partial(latent_kernel, longest),
            shape((blocks * longest, latent_width), BF),
            lengths,
            placement,
            tokens_t,
            w_latent,
            in_specs=[smem, smem, vmem, vmem],
            scratch=[
                pltpu.VMEM((blocks * longest, rows), BF),
                pltpu.SMEM((blocks,), jnp.int32),
            ],
            flops=2 * rows * latent_width * (width + blocks * longest),
            moved=2 * latent_width * (width + blocks * longest),
        )
        summed = lax.psum_scatter(picked, "dp", scatter_dimension=0, tiled=True)
    with jax.named_scope("up"):
        partial = call(
            functools.partial(up_kernel, lanes),
            shape((total_slots, 2 * hidden_units), BF),
            arrived,
            w_gate_up,
            scratch=[pltpu.VMEM((lanes * slots, width), BF)],
            flops=4 * total_slots * width * hidden_units,
            moved=4 * hidden_units * (residents * width + total_slots),
        )
        shares = exchange(partial.reshape(blocks, share, 2 * hidden_units), "dp")
        shares, summed = lax.optimization_barrier((shares, summed))

    with jax.named_scope("latent"):
        latent_cache = call(
            norm_kernel,
            shape((longest, latent_width), BF),
            summed,
            latent_gain.reshape(1, latent_width),
            flops=8 * longest * latent_width,
            moved=4 * longest * latent_width,
        )

    with jax.named_scope("gates"):
        gates = call(
            functools.partial(weights_kernel, residents, lanes),
            [shape((residents * lanes, slots, rows), BF)] * 2,
            routes_t,
            gates_t,
            flops=8 * experts * experts * rows,
            moved=8 * lanes * slots * rows,
        )

    with jax.named_scope("hidden"):
        hidden = call(
            hidden_kernel,
            shape((blocks, share, hidden_units), BF),
            shares,
            flops=2 * total_slots * hidden_units,
            moved=6 * total_slots * hidden_units,
        )
        gathered = exchange(hidden, "dp")
    with jax.named_scope("down"):
        produced = call(
            functools.partial(down_kernel, lanes),
            shape((slots, row), BF),
            gathered.reshape(total_slots, hidden_units),
            down_t,
            flops=2 * total_slots * width * hidden_units,
            moved=2 * hidden_units * (residents * width + total_slots),
        )
        back = exchange(produced.reshape(groups, 2, row), SE).reshape(slots, row)

    with jax.named_scope("mix"):
        mixed = call(
            mix_kernel,
            shape((width, rows), BF),
            back,
            *gates,
            flops=4 * total_slots * width * rows,
            moved=2 * total_slots * (width + 2 * rows),
        )
    return (mixed.T, latent_cache.reshape(1, 1, longest, latent_width))


def solution(mesh):
    return jax.shard_map(
        body,
        mesh=mesh,
        in_specs=(
            P(SE, "dp"),
            P(SE, None),
            P(SE, None),
            P(SE, "dp", None),
            P(SE, None, "dp"),
            P("dp", None),
            P(),
            P(SE, None),
            P(SE, None),
        ),
        out_specs=(P(SE, "dp"), P("dp", SE, None, None)),
        check_vma=False,
    )
```

```python
import functools

import jax
import jax.numpy as jnp
from jax import lax
from jax.experimental import pallas as pl
from jax.experimental.pallas import tpu as pltpu
from jax.sharding import PartitionSpec as P

SE = ("section", "expert")
NT = (((1,), (1,)), ((), ()))
TN = (((0,), (0,)), ((), ()))
BF = jnp.bfloat16
F32 = jnp.float32


def call(kernel, out_shape, *args, in_specs=None, scratch=(), flops=0, moved=0):
    kwargs = {}
    if in_specs is not None:
        kwargs["in_specs"] = in_specs
        kwargs["grid"] = (1,)
    return pl.pallas_call(
        kernel,
        out_shape=out_shape,
        scratch_shapes=list(scratch),
        cost_estimate=pl.CostEstimate(flops=flops, bytes_accessed=moved, transcendentals=0),
        compiler_params=pltpu.CompilerParams(vmem_limit_bytes=24 * 1024 * 1024),
        **kwargs,
    )(*args)


def iota(shape, dim):
    return lax.broadcasted_iota(jnp.int32, shape, dim)


def slot_rows(routes, ids, half):
    named, rank = [], []
    for g, routes_t in enumerate(routes):
        tops, rows = routes_t.shape
        hits = jnp.zeros((ids.shape[0], rows), F32)
        for k in range(tops):
            hits = hits + jnp.where(routes_t[k : k + 1, :] == ids, 1.0, 0.0)
        hits = jnp.where(half == g, hits, 0.0)
        earlier = (iota((rows, rows), 0) < iota((rows, rows), 1)).astype(F32).astype(BF)
        named.append(hits)
        rank.append(jnp.dot(hits.astype(BF), earlier, preferred_element_type=F32))
    return jnp.concatenate(named, axis=1), jnp.concatenate(rank, axis=1)


def slot_masks(named, rank, lanes):
    base = ((iota(named.shape, 0) & 1) * lanes).astype(F32)
    return [(named > 0.5) & (rank == base + float(i)) for i in range(lanes)]


def half_of(slot_rows_count):
    return (iota((slot_rows_count, 1), 0) >> 2) & 1


def dispatch_kernel(lanes, ids_ref, own_ref, other_ref, own_tokens, other_tokens, *outs):
    width = own_tokens.shape[0]
    ids = ids_ref[...]
    named, rank = slot_rows((own_ref[...], other_ref[...]), ids, half_of(ids.shape[0]))
    both = jnp.concatenate([own_tokens[...], other_tokens[...]], axis=1)
    for i, mask in enumerate(slot_masks(named, rank, lanes)):
        rows = lax.dot_general(mask.astype(F32).astype(BF), both, NT, preferred_element_type=F32)
        for d, out in enumerate(outs):
            out[:, i * width : (i + 1) * width] = rows[d * 8 : d * 8 + 8, :].astype(BF)


def weights_kernel(lanes, ids_ref, own_ref, other_ref, own_gates, other_gates, high_ref, low_ref):
    ids = ids_ref[...]
    routes = (own_ref[...], other_ref[...])
    named, rank = slot_rows(routes, ids, half_of(ids.shape[0]))
    gates = []
    for routes_t, weights_t in zip(routes, (own_gates[...], other_gates[...])):
        total = jnp.zeros((ids.shape[0], routes_t.shape[1]), F32)
        for k in range(routes_t.shape[0]):
            hit = routes_t[k : k + 1, :] == ids
            total = total + jnp.where(hit, weights_t[k : k + 1, :], 0.0)
        gates.append(total)
    gates = jnp.concatenate(gates, axis=1)
    high = gates.astype(BF).astype(F32)
    low = gates - high
    for i, mask in enumerate(slot_masks(named, rank, lanes)):
        high_ref[i] = jnp.where(mask, high, 0.0).astype(BF)
        low_ref[i] = jnp.where(mask, low, 0.0).astype(BF)


def by_expert(count):
    a = iota((count, count), 1)
    to = ((a >> 1) & 1) * (count // 2) + (a >> 3) * 4 + ((a >> 2) & 1) * 2 + (a & 1)
    return (iota((count, count), 0) == to).astype(F32).astype(BF)


def up_kernel(lanes, *refs):
    blocks, (weight_ref, out, gathered, packed) = refs[:-4], refs[-4:]
    count = gathered.shape[0]
    residents, width, columns = weight_ref.shape
    each, half = out.shape[0] // residents, count // residents
    step = 512 if columns % 512 == 0 else columns
    for d, block in enumerate(blocks):
        gathered[d * 8 : d * 8 + 8, :] = block[...].astype(F32)
    rows = jnp.dot(by_expert(count), gathered[...].astype(BF), preferred_element_type=F32)
    rows = rows.astype(BF)
    for r in range(residents):
        for i in range(lanes):
            piece = rows[r * half : (r + 1) * half, i * width : (i + 1) * width]
            packed[i * half : (i + 1) * half, :] = piece
        for c in range(0, columns, step):
            part = jnp.dot(
                packed[...], weight_ref[r, :, c : c + step], preferred_element_type=F32
            )
            out[r * each : (r + 1) * each, c : c + step] = part.astype(BF)


def hidden_kernel(parts_ref, out):
    blocks = parts_ref.shape[0]
    half = out.shape[2]
    total = parts_ref[0].astype(F32)
    for b in range(1, blocks):
        total = total + parts_ref[b].astype(F32)
    gate, up = total[:, :half], total[:, half:]
    hidden = (gate / (1.0 + jnp.exp(-gate)) * up).astype(BF)
    for b in range(blocks):
        out[b] = hidden


def down_kernel(lanes, hidden_ref, weight_ref, *refs):
    outs, packed = refs[:-1], refs[-1]
    count = packed.shape[0]
    residents, width, _ = weight_ref.shape
    each, half = hidden_ref.shape[0] // residents, count // residents
    for r in range(residents):
        part = lax.dot_general(
            hidden_ref[r * each : (r + 1) * each, :],
            weight_ref[r],
            NT,
            preferred_element_type=F32,
        ).astype(BF)
        for i in range(lanes):
            piece = part[i * half : (i + 1) * half, :]
            packed[r * half : (r + 1) * half, i * width : (i + 1) * width] = piece
    rows = lax.dot_general(by_expert(count), packed[...], TN, preferred_element_type=F32)
    for d, out in enumerate(outs):
        out[...] = rows[d * 8 : d * 8 + 8, :].astype(BF)


def mix_kernel(lanes, last, *refs):
    if last:
        blocks, (high_ref, low_ref, before_ref, own_ref, other_ref, gathered) = refs[:-6], refs[-6:]
        total = before_ref[...]
    else:
        blocks, (high_ref, low_ref, out, gathered) = refs[:-4], refs[-4:]
        total = jnp.zeros(out.shape, F32)
    width = total.shape[0]
    for d, block in enumerate(blocks):
        gathered[d * 8 : d * 8 + 8, :] = block[...].astype(F32)
    for i in range(lanes):
        rows = gathered[:, i * width : (i + 1) * width].astype(BF)
        total = total + lax.dot_general(rows, high_ref[i], TN, preferred_element_type=F32)
        total = total + lax.dot_general(rows, low_ref[i], TN, preferred_element_type=F32)
    if last:
        tokens = own_ref.shape[1]
        own_ref[...] = total[:, :tokens]
        other_ref[...] = total[:, tokens:].astype(BF)
    else:
        out[...] = total


def join_kernel(own_ref, other_ref, out):
    out[...] = (own_ref[...] + other_ref[...].astype(F32)).astype(BF)


def latent_kernel(longest, lengths_ref, placement_ref, tokens_ref, weight_ref, out, select, offset):
    requests = lengths_ref.shape[1]
    rows = tokens_ref.shape[1]
    partial = lax.dot_general(tokens_ref[...], weight_ref[...], TN, preferred_element_type=F32)
    run = jnp.int32(0)
    for j in range(requests):
        offset[j] = run
        run = run + lengths_ref[0, j]
    place, position = iota((longest, rows), 0), iota((longest, rows), 1)
    for q in range(requests):
        request = placement_ref[0, q]
        hit = (position == place + offset[request]) & (place < lengths_ref[0, request])
        select[q * longest : (q + 1) * longest, :] = hit.astype(F32).astype(BF)
    picked = jnp.dot(select[...], partial.astype(BF), preferred_element_type=F32)
    out[...] = picked.astype(BF)


def norm_kernel(parts_ref, gain_ref, out):
    total = parts_ref[0].astype(F32)
    for b in range(1, parts_ref.shape[0]):
        total = total + parts_ref[b].astype(F32)
    scale = lax.rsqrt(jnp.mean(total * total, axis=1, keepdims=True) + 1e-06)
    out[...] = (total * scale * gain_ref[...]).astype(BF)


def exchange(x, axes):
    return lax.all_to_all(x, axes, split_axis=0, concat_axis=0, tiled=True)


def swap(x):
    return lax.ppermute(x, "section", [(0, 1), (1, 0)])


def shift(x, distance, size):
    if distance % size == 0:
        return x
    return lax.ppermute(x, "expert", [(i, (i + distance) % size) for i in range(size)])


def distances(size):
    order = sorted(range(-((size - 1) // 2), size // 2 + 1), key=lambda d: (-abs(d), -d))
    return [d for d in order if d % 2 == 0], [d for d in order if d % 2]


def body(
    tokens, routes, route_weights, w_gate_up, w_down, w_latent, latent_gain, lengths, placement
):
    sections, ring = lax.axis_size("section"), lax.axis_size("expert")
    groups = sections * ring
    blocks = lax.axis_size("dp")
    rows, width = tokens.shape
    tops = routes.shape[1]
    residents = w_gate_up.shape[0]
    hidden_units = w_down.shape[1]
    latent_width = w_latent.shape[1]
    experts = residents * groups
    capacity = 5 * rows * tops // (4 * experts)
    lanes = capacity // 2
    longest = 2 * rows // blocks
    row = lanes * width
    shape = jax.ShapeDtypeStruct
    tokens_t, routes_t, gates_t = tokens.T, routes.T, route_weights.T
    down_t = w_down.transpose(0, 2, 1)
    vmem = pl.BlockSpec(memory_space=pltpu.VMEM)
    smem = pl.BlockSpec(memory_space=pltpu.SMEM)
    chunks = distances(ring)
    slots = 4 * residents * len(chunks[0])
    total_slots = slots * lanes
    share = total_slots // blocks

    with jax.named_scope("swap"):
        other_tokens, other_routes, other_gates = swap(tokens_t), swap(routes_t), swap(gates_t)

    with jax.named_scope("dispatch"):
        here = lax.axis_index("expert")
        first = lax.axis_index("section") * (experts // sections)
        local = experts // sections
        ids, sent = [], []
        for chunk in chunks:
            relative = [residents * d + r for d in chunk for h in range(2) for r in (0, 1) for j in (0, 1)]
            relative = jnp.asarray(relative, jnp.int32)[:, None]
            ids.append(first + (relative + residents * here + local) % local)
        for chunk, of_rows in zip(chunks, ids):
            sent.append(
                call(
                    functools.partial(dispatch_kernel, lanes),
                    [shape((8, row), BF)] * len(chunk),
                    of_rows,
                    routes_t,
                    other_routes,
                    tokens_t,
                    other_tokens,
                    flops=4 * rows * width * total_slots,
                    moved=2 * total_slots * width,
                )
            )
        arrived = [
            [shift(x, d, ring) for x, d in zip(of_chunk, chunk)]
            for of_chunk, chunk in zip(sent, chunks)
        ]

    with jax.named_scope("gates"):
        gates = [
            call(
                functools.partial(weights_kernel, lanes),
                [shape((lanes, slots, 2 * rows), BF)] * 2,
                of_rows,
                routes_t,
                other_routes,
                gates_t,
                other_gates,
                flops=4 * slots * rows * rows,
                moved=8 * total_slots * rows,
            )
            for of_rows in ids
        ]

    def up(c):
        with jax.named_scope("up"):
            return call(
                functools.partial(up_kernel, lanes),
                shape((total_slots, 2 * hidden_units), BF),
                *arrived[c],
                w_gate_up,
                scratch=[
                    pltpu.VMEM((slots, row), F32),
                    pltpu.VMEM((total_slots // residents, width), BF),
                ],
                flops=4 * total_slots * width * hidden_units,
                moved=4 * hidden_units * (residents * width + total_slots),
            )

    def middle(partial, beside):
        cut = 5 * len(beside) // 8
        with jax.named_scope("hidden"):
            shares = exchange(partial.reshape(blocks, share, 2 * hidden_units), "dp")
            shares, beside[:cut] = lax.optimization_barrier((shares, beside[:cut]))
            hidden = call(
                hidden_kernel,
                shape((blocks, share, hidden_units), BF),
                shares,
                flops=2 * total_slots * hidden_units,
                moved=6 * total_slots * hidden_units,
            )
            gathered = exchange(hidden, "dp")
            gathered, beside[cut:] = lax.optimization_barrier((gathered, beside[cut:]))
        return gathered

    def down(c, gathered):
        with jax.named_scope("down"):
            produced = call(
                functools.partial(down_kernel, lanes),
                [shape((8, row), BF)] * len(chunks[c]),
                gathered.reshape(total_slots, hidden_units),
                down_t,
                scratch=[pltpu.VMEM((slots, row), BF)],
                flops=2 * total_slots * width * hidden_units,
                moved=2 * hidden_units * (residents * width + total_slots),
            )
            return [shift(x, -d, ring) for x, d in zip(produced, chunks[c])]

    def mix(c, back, before):
        last = before is not None
        whole = shape((width, 2 * rows), F32)
        ends = [shape((width, rows), F32), shape((width, rows), BF)]
        with jax.named_scope("mix"):
            return call(
                functools.partial(mix_kernel, lanes, last),
                ends if last else whole,
                *back,
                *gates[c],
                *([before] if last else []),
                scratch=[pltpu.VMEM((slots, row), F32)],
                flops=8 * total_slots * width * rows,
                moved=4 * total_slots * (width + 2 * rows),
            )

    gathered = middle(up(0), arrived[1])
    partial, gathered = lax.optimization_barrier((up(1), gathered))
    back = down(0, gathered)
    gathered = middle(partial, back)
    gathered, late_tokens = lax.optimization_barrier((gathered, tokens_t))

    with jax.named_scope("latent"):
        picked = call(
            functools.partial(latent_kernel, longest),
            shape((blocks * longest, latent_width), BF),
            lengths,
            placement,
            late_tokens,
            w_latent,
            in_specs=[smem, smem, vmem, vmem],
            scratch=[
                pltpu.VMEM((blocks * longest, rows), BF),
                pltpu.SMEM((blocks,), jnp.int32),
            ],
            flops=2 * rows * latent_width * (width + blocks * longest),
            moved=2 * latent_width * (width + blocks * longest),
        )
        received = exchange(picked.reshape(blocks, longest, latent_width), "dp")
        latent_cache = call(
            norm_kernel,
            shape((longest, latent_width), BF),
            received,
            latent_gain.reshape(1, latent_width),
            flops=blocks * longest * latent_width,
            moved=2 * blocks * longest * latent_width,
        )

    total = mix(0, back, None)
    total = mix(1, down(1, gathered), total)
    with jax.named_scope("join"):
        own, other = total
        mixed = call(
            join_kernel,
            shape((width, rows), BF),
            own,
            swap(other),
            flops=width * rows,
            moved=8 * width * rows,
        )
    return (mixed.T, latent_cache.reshape(1, 1, longest, latent_width))


def solution(mesh):
    return jax.shard_map(
        body,
        mesh=mesh,
        in_specs=(
            P(SE, "dp"),
            P(SE, None),
            P(SE, None),
            P(SE, "dp", None),
            P(SE, None, "dp"),
            P("dp", None),
            P(),
            P(SE, None),
            P(SE, None),
        ),
        out_specs=(P(SE, "dp"), P("dp", SE, None, None)),
        check_vma=False,
    )
```

```python
import functools

import jax
import jax.numpy as jnp
from jax import lax
from jax.experimental import pallas as pl
from jax.experimental.pallas import tpu as pltpu
from jax.sharding import PartitionSpec as P

SE = ("section", "expert")
NT = (((1,), (1,)), ((), ()))
TN = (((0,), (0,)), ((), ()))
BF = jnp.bfloat16
F32 = jnp.float32


def call(kernel, out_shape, *args, in_specs=None, scratch=(), flops=0, moved=0):
    kwargs = {}
    if in_specs is not None:
        kwargs["in_specs"] = in_specs
        kwargs["grid"] = (1,)
    return pl.pallas_call(
        kernel,
        out_shape=out_shape,
        scratch_shapes=list(scratch),
        cost_estimate=pl.CostEstimate(flops=flops, bytes_accessed=moved, transcendentals=0),
        compiler_params=pltpu.CompilerParams(vmem_limit_bytes=24 * 1024 * 1024),
        **kwargs,
    )(*args)


def iota(shape, dim):
    return lax.broadcasted_iota(jnp.int32, shape, dim)


def slot_masks(pick_ref, routes_t, lanes, slot_count):
    tops, rows = routes_t.shape
    resident, part = pick_ref[0], pick_ref[1]
    ids = (iota((slot_count, rows), 0) >> 1) * 2 + resident
    named = jnp.zeros((slot_count, rows), F32)
    for k in range(tops):
        named = named + jnp.where(routes_t[k : k + 1, :] == ids, 1.0, 0.0)
    earlier = (iota((rows, rows), 0) < iota((rows, rows), 1)).astype(F32).astype(BF)
    rank = jnp.dot(named.astype(BF), earlier, preferred_element_type=F32)
    base = (part * lanes).astype(F32)
    return ids, [(named > 0.5) & (rank == base + float(i)) for i in range(lanes)]


def by_half(x):
    half = iota(x.shape, 0) & 1
    return jnp.concatenate([jnp.where(half == 0, x, 0.0), jnp.where(half == 1, x, 0.0)], axis=1)


def dispatch_kernel(lanes, pick_ref, routes_ref, t0, t1, t2, t3, out):
    span = 2 * t0.shape[0]
    _, masks = slot_masks(pick_ref, routes_ref[...], lanes, out.shape[0])
    left = jnp.concatenate([t0[...], t1[...]], axis=0)
    right = jnp.concatenate([t2[...], t3[...]], axis=0)
    both = jnp.concatenate([left, right], axis=1)
    for i, mask in enumerate(masks):
        hot = by_half(mask.astype(F32)).astype(BF)
        rows = lax.dot_general(hot, both, NT, preferred_element_type=F32)
        out[:, i * span : (i + 1) * span] = rows.astype(BF)


def weights_kernel(lanes, pick_ref, routes_ref, weights_ref, high_ref, low_ref):
    routes_t, weights_t = routes_ref[...], weights_ref[...]
    ids, masks = slot_masks(pick_ref, routes_t, lanes, high_ref.shape[1])
    gates = jnp.zeros(ids.shape, F32)
    for k in range(routes_t.shape[0]):
        gates = gates + jnp.where(routes_t[k : k + 1, :] == ids, weights_t[k : k + 1, :], 0.0)
    high = gates.astype(BF).astype(F32)
    low = gates - high
    for i, mask in enumerate(masks):
        high_ref[i] = by_half(jnp.where(mask, high, 0.0)).astype(BF)
        low_ref[i] = by_half(jnp.where(mask, low, 0.0)).astype(BF)


def halves_first(count):
    a = iota((count, count), 1)
    return (iota((count, count), 0) == (a & 1) * (count // 2) + (a >> 1)).astype(F32).astype(BF)


def up_kernel(lanes, rows_ref, w0, w1, w2, w3, out, packed):
    count = rows_ref.shape[0]
    groups = count // 2
    width, columns = w0.shape
    span = 2 * width
    step = 512 if columns % 512 == 0 else columns
    rows = jnp.dot(halves_first(count), rows_ref[...], preferred_element_type=F32).astype(BF)
    for i in range(lanes):
        for p in range(2):
            piece = rows[p * groups : (p + 1) * groups, i * span : (i + 1) * span]
            packed[i * groups : (i + 1) * groups, p * span : (p + 1) * span] = piece
    for c in range(0, columns, step):
        total = None
        for k, weight in enumerate((w0, w1, w2, w3)):
            part = jnp.dot(
                packed[:, k * width : (k + 1) * width],
                weight[:, c : c + step],
                preferred_element_type=F32,
            )
            total = part if total is None else total + part
        out[:, c : c + step] = total.astype(BF)


def hidden_kernel(parts_ref, out):
    blocks = parts_ref.shape[0]
    half = out.shape[2]
    total = parts_ref[0].astype(F32)
    for b in range(1, blocks):
        total = total + parts_ref[b].astype(F32)
    gate, up = total[:, :half], total[:, half:]
    hidden = (gate / (1.0 + jnp.exp(-gate)) * up).astype(BF)
    for b in range(blocks):
        out[b] = hidden


def down_kernel(lanes, hidden_ref, w0, w1, w2, w3, out, packed):
    count = out.shape[0]
    groups = count // 2
    width = w0.shape[0]
    span = 2 * width
    for k, weight in enumerate((w0, w1, w2, w3)):
        part = lax.dot_general(hidden_ref[...], weight[...], NT, preferred_element_type=F32)
        part = part.astype(BF)
        p, skip = k // 2, (k % 2) * width
        for i in range(lanes):
            at = i * span + skip
            piece = part[i * groups : (i + 1) * groups, :]
            packed[p * groups : (p + 1) * groups, at : at + width] = piece
    rows = lax.dot_general(halves_first(count), packed[...], TN, preferred_element_type=F32)
    out[...] = rows.astype(BF)


def mix_kernel(lanes, back_ref, high_ref, low_ref, own_ref, o1, o2, o3):
    width, tokens = own_ref.shape
    span = 2 * width
    total = jnp.zeros((span, 2 * tokens), F32)
    for i in range(lanes):
        rows = back_ref[:, i * span : (i + 1) * span]
        total = total + lax.dot_general(rows, high_ref[i], TN, preferred_element_type=F32)
        total = total + lax.dot_general(rows, low_ref[i], TN, preferred_element_type=F32)
    own_ref[...] = total[:width, :tokens]
    o1[...] = total[width:, :tokens].astype(BF)
    o2[...] = total[:width, tokens:].astype(BF)
    o3[...] = total[width:, tokens:].astype(BF)


def join_kernel(own_ref, a_ref, b_ref, c_ref, out):
    total = own_ref[...] + a_ref[...].astype(F32) + b_ref[...].astype(F32)
    out[...] = (total + c_ref[...].astype(F32)).astype(BF)


def latent_kernel(longest, lengths_ref, placement_ref, tokens_ref, weight_ref, out, select, offset):
    requests = lengths_ref.shape[1]
    rows = tokens_ref.shape[1]
    partial = lax.dot_general(tokens_ref[...], weight_ref[...], TN, preferred_element_type=F32)
    run = jnp.int32(0)
    for j in range(requests):
        offset[j] = run
        run = run + lengths_ref[0, j]
    place, position = iota((longest, rows), 0), iota((longest, rows), 1)
    for q in range(requests):
        request = placement_ref[0, q]
        hit = (position == place + offset[request]) & (place < lengths_ref[0, request])
        select[q * longest : (q + 1) * longest, :] = hit.astype(F32).astype(BF)
    picked = jnp.dot(select[...], partial.astype(BF), preferred_element_type=F32)
    out[...] = picked.astype(BF)


def norm_kernel(sum_ref, gain_ref, out):
    total = sum_ref[...]
    scale = lax.rsqrt(jnp.mean(total * total, axis=1, keepdims=True) + 1e-06)
    out[...] = (total * scale * gain_ref[...]).astype(BF)


def exchange(x, axes, groups=None):
    return lax.all_to_all(x, axes, split_axis=0, concat_axis=0, axis_index_groups=groups, tiled=True)


def flip(x, bits):
    return lax.ppermute(x, "dp", [(i, i ^ bits) for i in range(lax.axis_size("dp"))])


def gather_expert(array, resident):
    own = lax.dynamic_index_in_dim(array, resident, 0, keepdims=False)
    cross = lax.dynamic_index_in_dim(array, 1 - resident, 0, keepdims=False)
    second, third = flip(own, 1), flip(cross, 3)
    return own, second, third, flip(third, 1)


def sum_to_owner(parts):
    me = lax.axis_index("dp")
    bit = parts.shape[0] // 2
    while bit:
        high = (me & bit) != 0
        keep = jnp.where(high, parts[bit:], parts[:bit])
        send = jnp.where(high, parts[:bit], parts[bit:])
        parts = keep.astype(F32) + flip(send, bit).astype(F32)
        bit //= 2
        if bit:
            parts = parts.astype(BF)
    return parts[0]


def body(
    tokens, routes, route_weights, w_gate_up, w_down, w_latent, latent_gain, lengths, placement
):
    groups = lax.axis_size(SE)
    blocks = lax.axis_size("dp")
    along_y = 4
    along_x = blocks // along_y
    columns = [[y + along_y * x for x in range(along_x)] for y in range(along_y)]
    rows, width = tokens.shape
    tops = routes.shape[1]
    residents = w_gate_up.shape[0]
    hidden_units = w_down.shape[1]
    latent_width = w_latent.shape[1]
    experts = residents * groups
    capacity = 5 * rows * tops // (4 * experts)
    lanes = capacity // 2
    longest = 2 * rows // blocks
    slots = 2 * groups
    row = 2 * lanes * width
    taken = lanes * groups
    share = taken // along_x
    shape = jax.ShapeDtypeStruct
    tokens_t, routes_t, gates_t = tokens.T, routes.T, route_weights.T
    vmem = pl.BlockSpec(memory_space=pltpu.VMEM)
    smem = pl.BlockSpec(memory_space=pltpu.SMEM)

    at_y = lax.axis_index("dp") % along_y
    resident = at_y // 2
    pick = jnp.stack([resident, at_y % 2])

    with jax.named_scope("tokens"):
        pieces = [tokens_t, flip(tokens_t, 1), flip(tokens_t, 3), flip(tokens_t, 2)]

    with jax.named_scope("dispatch"):
        outgoing = call(
            functools.partial(dispatch_kernel, lanes),
            shape((slots, row), BF),
            pick,
            routes_t,
            *pieces,
            in_specs=[smem] + [vmem] * 5,
            flops=8 * slots * rows * width * lanes,
            moved=2 * slots * row,
        )
        outgoing, w_gate_up, w_down = lax.optimization_barrier((outgoing, w_gate_up, w_down))
        arrived = exchange(outgoing.reshape(groups, 2, row), SE)

    with jax.named_scope("gather"):
        up_blocks = gather_expert(w_gate_up, resident)
        down_blocks = gather_expert(w_down.transpose(0, 2, 1), resident)
        arrived, up_blocks, down_blocks = lax.optimization_barrier(
            (arrived, up_blocks, down_blocks)
        )

    with jax.named_scope("up"):
        partial = call(
            functools.partial(up_kernel, lanes),
            shape((taken, 2 * hidden_units), BF),
            arrived.reshape(slots, row),
            *up_blocks,
            scratch=[pltpu.VMEM((taken, 4 * width), BF)],
            flops=16 * taken * width * hidden_units,
            moved=4 * hidden_units * (4 * width + taken),
        )
        shares = exchange(partial.reshape(along_x, share, 2 * hidden_units), "dp", columns)

    with jax.named_scope("hidden"):
        hidden = call(
            hidden_kernel,
            shape((along_x, share, hidden_units), BF),
            shares,
            flops=2 * taken * hidden_units,
            moved=6 * taken * hidden_units,
        )
        gathered = exchange(hidden, "dp", columns)

    with jax.named_scope("down"):
        produced = call(
            functools.partial(down_kernel, lanes),
            shape((slots, row), BF),
            gathered.reshape(taken, hidden_units),
            *down_blocks,
            scratch=[pltpu.VMEM((slots, row), BF)],
            flops=8 * taken * width * hidden_units,
            moved=2 * hidden_units * (4 * width + taken),
        )
        produced, tokens_t, gates_t = lax.optimization_barrier((produced, tokens_t, gates_t))
        back = exchange(produced.reshape(groups, 2, row), SE).reshape(slots, row)

    with jax.named_scope("gates"):
        gates = call(
            functools.partial(weights_kernel, lanes),
            [shape((lanes, slots, 2 * rows), BF)] * 2,
            pick,
            routes_t,
            gates_t,
            in_specs=[smem, vmem, vmem],
            flops=4 * slots * rows * rows,
            moved=8 * lanes * slots * rows,
        )

    with jax.named_scope("latent"):
        picked = call(
            functools.partial(latent_kernel, longest),
            shape((blocks * longest, latent_width), BF),
            lengths,
            placement,
            tokens_t,
            w_latent,
            in_specs=[smem, smem, vmem, vmem],
            scratch=[
                pltpu.VMEM((blocks * longest, rows), BF),
                pltpu.SMEM((blocks,), jnp.int32),
            ],
            flops=2 * rows * latent_width * (width + blocks * longest),
            moved=2 * latent_width * (width + blocks * longest),
        )
        latent = sum_to_owner(picked.reshape(blocks, longest, latent_width))
        latent_cache = call(
            norm_kernel,
            shape((longest, latent_width), BF),
            latent,
            latent_gain.reshape(1, latent_width),
            flops=8 * longest * latent_width,
            moved=4 * longest * latent_width,
        )
        back, latent_cache = lax.optimization_barrier((back, latent_cache))

    with jax.named_scope("mix"):
        own, *others = call(
            functools.partial(mix_kernel, lanes),
            [shape((width, rows), F32)] + [shape((width, rows), BF)] * 3,
            back,
            *gates,
            flops=32 * taken * width * rows,
            moved=2 * slots * row + 8 * lanes * slots * rows,
        )
        mixed = call(
            join_kernel,
            shape((width, rows), BF),
            own,
            *[flip(x, bits) for x, bits in zip(others, (1, 3, 2))],
            flops=3 * width * rows,
            moved=12 * width * rows,
        )
    return (mixed.T, latent_cache.reshape(1, 1, longest, latent_width))


def solution(mesh):
    return jax.shard_map(
        body,
        mesh=mesh,
        in_specs=(
            P(SE, "dp"),
            P(SE, None),
            P(SE, None),
            P(SE, "dp", None),
            P(SE, None, "dp"),
            P("dp", None),
            P(),
            P(SE, None),
            P(SE, None),
        ),
        out_specs=(P(SE, "dp"), P("dp", SE, None, None)),
        check_vma=False,
    )
```

```python
import functools

import jax
import jax.numpy as jnp
from jax import lax
from jax.experimental import pallas as pl
from jax.experimental.pallas import tpu as pltpu
from jax.sharding import PartitionSpec as P

SE = ("section", "expert")
NT = (((1,), (1,)), ((), ()))
TN = (((0,), (0,)), ((), ()))
BF = jnp.bfloat16
F32 = jnp.float32


def call(kernel, out_shape, *args, in_specs=None, scratch=(), flops=0, moved=0):
    kwargs = {}
    if in_specs is not None:
        kwargs["in_specs"] = in_specs
        kwargs["grid"] = (1,)
    return pl.pallas_call(
        kernel,
        out_shape=out_shape,
        scratch_shapes=list(scratch),
        cost_estimate=pl.CostEstimate(flops=flops, bytes_accessed=moved, transcendentals=0),
        compiler_params=pltpu.CompilerParams(vmem_limit_bytes=24 * 1024 * 1024),
        **kwargs,
    )(*args)


def iota(shape, dim):
    return lax.broadcasted_iota(jnp.int32, shape, dim)


def slot_masks(pick_ref, routes_t, lanes, slot_count):
    tops, rows = routes_t.shape
    resident, part = pick_ref[0], pick_ref[1]
    ids = (iota((slot_count, rows), 0) >> 1) * 2 + resident
    named = jnp.zeros((slot_count, rows), F32)
    for k in range(tops):
        named = named + jnp.where(routes_t[k : k + 1, :] == ids, 1.0, 0.0)
    earlier = (iota((rows, rows), 0) < iota((rows, rows), 1)).astype(F32).astype(BF)
    rank = jnp.dot(named.astype(BF), earlier, preferred_element_type=F32)
    base = (part * lanes).astype(F32)
    return ids, [(named > 0.5) & (rank == base + float(i)) for i in range(lanes)]


def by_half(x):
    half = iota(x.shape, 0) & 1
    return jnp.concatenate([jnp.where(half == 0, x, 0.0), jnp.where(half == 1, x, 0.0)], axis=1)


def dispatch_kernel(lanes, pick_ref, routes_ref, t0, t1, t2, t3, out):
    span = 2 * t0.shape[0]
    _, masks = slot_masks(pick_ref, routes_ref[...], lanes, out.shape[0])
    left = jnp.concatenate([t0[...], t1[...]], axis=0)
    right = jnp.concatenate([t2[...], t3[...]], axis=0)
    both = jnp.concatenate([left, right], axis=1)
    for i, mask in enumerate(masks):
        hot = by_half(mask.astype(F32)).astype(BF)
        rows = lax.dot_general(hot, both, NT, preferred_element_type=F32)
        out[:, i * span : (i + 1) * span] = rows.astype(BF)


def weights_kernel(lanes, pick_ref, routes_ref, weights_ref, high_ref, low_ref):
    routes_t, weights_t = routes_ref[...], weights_ref[...]
    ids, masks = slot_masks(pick_ref, routes_t, lanes, high_ref.shape[1])
    gates = jnp.zeros(ids.shape, F32)
    for k in range(routes_t.shape[0]):
        gates = gates + jnp.where(routes_t[k : k + 1, :] == ids, weights_t[k : k + 1, :], 0.0)
    high = gates.astype(BF).astype(F32)
    low = gates - high
    for i, mask in enumerate(masks):
        high_ref[i] = by_half(jnp.where(mask, high, 0.0)).astype(BF)
        low_ref[i] = by_half(jnp.where(mask, low, 0.0)).astype(BF)


def halves_first(count):
    a = iota((count, count), 1)
    return (iota((count, count), 0) == (a & 1) * (count // 2) + (a >> 1)).astype(F32).astype(BF)


def up_kernel(lanes, rows_ref, w0, w1, w2, w3, out, packed):
    count = rows_ref.shape[0]
    groups = count // 2
    width, columns = w0.shape
    span = 2 * width
    step = 512 if columns % 512 == 0 else columns
    rows = jnp.dot(halves_first(count), rows_ref[...], preferred_element_type=F32).astype(BF)
    for i in range(lanes):
        for p in range(2):
            piece = rows[p * groups : (p + 1) * groups, i * span : (i + 1) * span]
            packed[i * groups : (i + 1) * groups, p * span : (p + 1) * span] = piece
    for c in range(0, columns, step):
        total = None
        for k, weight in enumerate((w0, w1, w2, w3)):
            part = jnp.dot(
                packed[:, k * width : (k + 1) * width],
                weight[:, c : c + step],
                preferred_element_type=F32,
            )
            total = part if total is None else total + part
        out[:, c : c + step] = total.astype(BF)


def hidden_kernel(parts_ref, out):
    blocks = parts_ref.shape[0]
    half = out.shape[2]
    total = parts_ref[0].astype(F32)
    for b in range(1, blocks):
        total = total + parts_ref[b].astype(F32)
    gate, up = total[:, :half], total[:, half:]
    hidden = (gate / (1.0 + jnp.exp(-gate)) * up).astype(BF)
    for b in range(blocks):
        out[b] = hidden


def down_kernel(lanes, hidden_ref, w0, w1, w2, w3, out, packed):
    count = out.shape[0]
    groups = count // 2
    width = w0.shape[0]
    span = 2 * width
    for k, weight in enumerate((w0, w1, w2, w3)):
        part = lax.dot_general(hidden_ref[...], weight[...], NT, preferred_element_type=F32)
        part = part.astype(BF)
        p, skip = k // 2, (k % 2) * width
        for i in range(lanes):
            at = i * span + skip
            piece = part[i * groups : (i + 1) * groups, :]
            packed[p * groups : (p + 1) * groups, at : at + width] = piece
    rows = lax.dot_general(halves_first(count), packed[...], TN, preferred_element_type=F32)
    out[...] = rows.astype(BF)


def mix_kernel(lanes, pick_ref, back_ref, high_ref, low_ref, out):
    _, width, tokens = out.shape
    span = 2 * width
    total = jnp.zeros((span, 2 * tokens), F32)
    for i in range(lanes):
        rows = back_ref[:, i * span : (i + 1) * span]
        total = total + lax.dot_general(rows, high_ref[i], TN, preferred_element_type=F32)
        total = total + lax.dot_general(rows, low_ref[i], TN, preferred_element_type=F32)
    place = pick_ref[2]
    for k in range(4):
        at, to = (k % 2) * width, (k // 2) * tokens
        out[place ^ k] = total[at : at + width, to : to + tokens].astype(BF)


def join_kernel(parts_ref, out):
    total = parts_ref[0].astype(F32)
    for k in range(1, parts_ref.shape[0]):
        total = total + parts_ref[k].astype(F32)
    out[...] = total.astype(BF)


def latent_kernel(longest, lengths_ref, placement_ref, tokens_ref, weight_ref, out, select, offset):
    requests = lengths_ref.shape[1]
    rows = tokens_ref.shape[1]
    partial = lax.dot_general(tokens_ref[...], weight_ref[...], TN, preferred_element_type=F32)
    run = jnp.int32(0)
    for j in range(requests):
        offset[j] = run
        run = run + lengths_ref[0, j]
    place, position = iota((longest, rows), 0), iota((longest, rows), 1)
    for q in range(requests):
        request = placement_ref[0, q]
        hit = (position == place + offset[request]) & (place < lengths_ref[0, request])
        select[q * longest : (q + 1) * longest, :] = hit.astype(F32).astype(BF)
    picked = jnp.dot(select[...], partial.astype(BF), preferred_element_type=F32)
    out[...] = picked.astype(BF)


def norm_kernel(sum_ref, gain_ref, out):
    total = sum_ref[...]
    scale = lax.rsqrt(jnp.mean(total * total, axis=1, keepdims=True) + 1e-06)
    out[...] = (total * scale * gain_ref[...]).astype(BF)


def exchange(x, axes, groups=None):
    return lax.all_to_all(x, axes, split_axis=0, concat_axis=0, axis_index_groups=groups, tiled=True)


def flip(x, bits):
    return lax.ppermute(x, "dp", [(i, i ^ bits) for i in range(lax.axis_size("dp"))])


def cosets(size, *flips):
    reach = [0]
    for bits in flips:
        reach += [i ^ bits for i in reach]
    return sorted({tuple(sorted(i ^ j for j in reach)) for i in range(size)})


def gather_expert(array, resident):
    own = lax.dynamic_index_in_dim(array, resident, 0, keepdims=False)
    cross = lax.dynamic_index_in_dim(array, 1 - resident, 0, keepdims=False)
    second, third = flip(own, 1), flip(cross, 4)
    return own, second, third, flip(third, 1)


def sum_to_owner(parts):
    me = lax.axis_index("dp")
    bit = parts.shape[0] // 2
    while bit:
        high = (me & bit) != 0
        keep = jnp.where(high, parts[bit:], parts[:bit])
        send = jnp.where(high, parts[:bit], parts[bit:])
        parts = keep.astype(F32) + flip(send, bit).astype(F32)
        bit //= 2
        if bit:
            parts = parts.astype(BF)
    return parts[0]


def body(
    tokens, routes, route_weights, w_gate_up, w_down, w_latent, latent_gain, lengths, placement
):
    groups = lax.axis_size(SE)
    blocks = lax.axis_size("dp")
    near, far = cosets(blocks, 1, 4), cosets(blocks, 3, 12)
    spread = len(far[0])
    rows, width = tokens.shape
    tops = routes.shape[1]
    residents = w_gate_up.shape[0]
    hidden_units = w_down.shape[1]
    latent_width = w_latent.shape[1]
    experts = residents * groups
    capacity = 5 * rows * tops // (4 * experts)
    lanes = capacity // 2
    longest = 2 * rows // blocks
    slots = 2 * groups
    row = 2 * lanes * width
    taken = lanes * groups
    share = taken // spread
    shape = jax.ShapeDtypeStruct
    tokens_t, routes_t, gates_t = tokens.T, routes.T, route_weights.T
    vmem = pl.BlockSpec(memory_space=pltpu.VMEM)
    smem = pl.BlockSpec(memory_space=pltpu.SMEM)

    here = lax.axis_index("dp")
    resident = ((here >> 2) ^ (here >> 3)) & 1
    place = ((here >> 1) & 2) + (here & 1)
    pick = jnp.stack([resident, (here ^ (here >> 1)) & 1, place])

    with jax.named_scope("tokens"):
        both = flip(tokens_t, 5)
        pieces = [tokens_t, flip(tokens_t, 1), flip(tokens_t, 4), both]

    with jax.named_scope("dispatch"):
        outgoing = call(
            functools.partial(dispatch_kernel, lanes),
            shape((slots, row), BF),
            pick,
            routes_t,
            *pieces,
            in_specs=[smem] + [vmem] * 5,
            flops=8 * slots * rows * width * lanes,
            moved=2 * slots * row,
        )
        outgoing, w_gate_up, w_down = lax.optimization_barrier((outgoing, w_gate_up, w_down))
        arrived = exchange(outgoing.reshape(groups, 2, row), SE)

    with jax.named_scope("gather"):
        up_blocks = gather_expert(w_gate_up, resident)
        down_blocks = gather_expert(w_down.transpose(0, 2, 1), resident)
        arrived, down_blocks = lax.optimization_barrier((arrived, down_blocks))

    with jax.named_scope("up"):
        partial = call(
            functools.partial(up_kernel, lanes),
            shape((taken, 2 * hidden_units), BF),
            arrived.reshape(slots, row),
            *up_blocks,
            scratch=[pltpu.VMEM((taken, 4 * width), BF)],
            flops=16 * taken * width * hidden_units,
            moved=4 * hidden_units * (4 * width + taken),
        )
        shares = exchange(partial.reshape(spread, share, 2 * hidden_units), "dp", far)

    with jax.named_scope("hidden"):
        hidden = call(
            hidden_kernel,
            shape((spread, share, hidden_units), BF),
            shares,
            flops=2 * taken * hidden_units,
            moved=6 * taken * hidden_units,
        )
        gathered = exchange(hidden, "dp", far)

    with jax.named_scope("down"):
        produced = call(
            functools.partial(down_kernel, lanes),
            shape((slots, row), BF),
            gathered.reshape(taken, hidden_units),
            *down_blocks,
            scratch=[pltpu.VMEM((slots, row), BF)],
            flops=8 * taken * width * hidden_units,
            moved=2 * hidden_units * (4 * width + taken),
        )
        produced, tokens_t, gates_t = lax.optimization_barrier((produced, tokens_t, gates_t))
        back = exchange(produced.reshape(groups, 2, row), SE).reshape(slots, row)

    with jax.named_scope("gates"):
        gates = call(
            functools.partial(weights_kernel, lanes),
            [shape((lanes, slots, 2 * rows), BF)] * 2,
            pick,
            routes_t,
            gates_t,
            in_specs=[smem, vmem, vmem],
            flops=4 * slots * rows * rows,
            moved=8 * lanes * slots * rows,
        )

    with jax.named_scope("latent"):
        picked = call(
            functools.partial(latent_kernel, longest),
            shape((blocks * longest, latent_width), BF),
            lengths,
            placement,
            tokens_t,
            w_latent,
            in_specs=[smem, smem, vmem, vmem],
            scratch=[
                pltpu.VMEM((blocks * longest, rows), BF),
                pltpu.SMEM((blocks,), jnp.int32),
            ],
            flops=2 * rows * latent_width * (width + blocks * longest),
            moved=2 * latent_width * (width + blocks * longest),
        )
        latent = sum_to_owner(picked.reshape(blocks, longest, latent_width))
        latent_cache = call(
            norm_kernel,
            shape((longest, latent_width), BF),
            latent,
            latent_gain.reshape(1, latent_width),
            flops=8 * longest * latent_width,
            moved=4 * longest * latent_width,
        )
        back, latent_cache = lax.optimization_barrier((back, latent_cache))

    with jax.named_scope("mix"):
        parts = call(
            functools.partial(mix_kernel, lanes),
            shape((4, width, rows), BF),
            pick,
            back,
            *gates,
            in_specs=[smem] + [vmem] * 3,
            flops=32 * taken * width * rows,
            moved=2 * slots * row + 8 * lanes * slots * rows,
        )
        mixed = call(
            join_kernel,
            shape((width, rows), BF),
            exchange(parts, "dp", near),
            flops=3 * width * rows,
            moved=10 * width * rows,
        )
    return (mixed.T, latent_cache.reshape(1, 1, longest, latent_width))


def solution(mesh):
    return jax.shard_map(
        body,
        mesh=mesh,
        in_specs=(
            P(SE, "dp"),
            P(SE, None),
            P(SE, None),
            P(SE, "dp", None),
            P(SE, None, "dp"),
            P("dp", None),
            P(),
            P(SE, None),
            P(SE, None),
        ),
        out_specs=(P(SE, "dp"), P("dp", SE, None, None)),
        check_vma=False,
    )
```

```python
import functools

import jax
import jax.numpy as jnp
from jax import lax
from jax.experimental import pallas as pl
from jax.experimental.pallas import tpu as pltpu
from jax.sharding import PartitionSpec as P

SE = ("section", "expert")
NT = (((1,), (1,)), ((), ()))
TN = (((0,), (0,)), ((), ()))
BF = jnp.bfloat16
F32 = jnp.float32


def call(kernel, out_shape, *args, in_specs=None, scratch=(), flops=0, moved=0):
    kwargs = {}
    if in_specs is not None:
        kwargs["in_specs"] = in_specs
        kwargs["grid"] = (1,)
    return pl.pallas_call(
        kernel,
        out_shape=out_shape,
        scratch_shapes=list(scratch),
        cost_estimate=pl.CostEstimate(flops=flops, bytes_accessed=moved, transcendentals=0),
        compiler_params=pltpu.CompilerParams(vmem_limit_bytes=24 * 1024 * 1024),
        **kwargs,
    )(*args)


def iota(shape, dim):
    return lax.broadcasted_iota(jnp.int32, shape, dim)


def slot_masks(pick_ref, routes_t, lanes, slot_count):
    tops, rows = routes_t.shape
    resident, part = pick_ref[0], pick_ref[1]
    ids = (iota((slot_count, rows), 0) >> 1) * 2 + resident
    named = jnp.zeros((slot_count, rows), F32)
    for k in range(tops):
        named = named + jnp.where(routes_t[k : k + 1, :] == ids, 1.0, 0.0)
    earlier = (iota((rows, rows), 0) < iota((rows, rows), 1)).astype(F32).astype(BF)
    rank = jnp.dot(named.astype(BF), earlier, preferred_element_type=F32)
    base = (part * lanes).astype(F32)
    return ids, [(named > 0.5) & (rank == base + float(i)) for i in range(lanes)]


def by_half(x):
    half = iota(x.shape, 0) & 1
    return jnp.concatenate([jnp.where(half == 0, x, 0.0), jnp.where(half == 1, x, 0.0)], axis=1)


def hot_kernel(lanes, pick_ref, routes_ref, tokens_ref, out, tokens_out):
    _, masks = slot_masks(pick_ref, routes_ref[...], lanes, out.shape[1])
    for i, mask in enumerate(masks):
        out[i] = by_half(mask.astype(F32)).astype(BF)
    tokens_out[...] = tokens_ref[...]


def dispatch_kernel(hot_ref, t0, t1, t2, t3, out):
    span = 2 * t0.shape[0]
    left = jnp.concatenate([t0[...], t1[...]], axis=0)
    right = jnp.concatenate([t2[...], t3[...]], axis=0)
    both = jnp.concatenate([left, right], axis=1)
    for i in range(hot_ref.shape[0]):
        rows = lax.dot_general(hot_ref[i], both, NT, preferred_element_type=F32)
        out[:, i * span : (i + 1) * span] = rows.astype(BF)


def weights_kernel(lanes, pick_ref, routes_ref, weights_ref, high_ref, low_ref):
    routes_t, weights_t = routes_ref[...], weights_ref[...]
    ids, masks = slot_masks(pick_ref, routes_t, lanes, high_ref.shape[1])
    gates = jnp.zeros(ids.shape, F32)
    for k in range(routes_t.shape[0]):
        gates = gates + jnp.where(routes_t[k : k + 1, :] == ids, weights_t[k : k + 1, :], 0.0)
    high = gates.astype(BF).astype(F32)
    low = gates - high
    for i, mask in enumerate(masks):
        high_ref[i] = by_half(jnp.where(mask, high, 0.0)).astype(BF)
        low_ref[i] = by_half(jnp.where(mask, low, 0.0)).astype(BF)


def halves_first(count):
    a = iota((count, count), 1)
    return (iota((count, count), 0) == (a & 1) * (count // 2) + (a >> 1)).astype(F32).astype(BF)


def up_kernel(lanes, rows_ref, w0, w1, w2, w3, out, packed):
    count = rows_ref.shape[0]
    groups = count // 2
    width = w0.shape[0]
    span = 2 * width

    @pl.when(pl.program_id(0) == 0)
    def _():
        rows = jnp.dot(halves_first(count), rows_ref[...], preferred_element_type=F32).astype(BF)
        for i in range(lanes):
            for p in range(2):
                piece = rows[p * groups : (p + 1) * groups, i * span : (i + 1) * span]
                packed[i * groups : (i + 1) * groups, p * span : (p + 1) * span] = piece

    total = jnp.zeros(out.shape, F32)
    for k, weight in enumerate((w0, w1, w2, w3)):
        rows = packed[:, k * width : (k + 1) * width]
        total = total + jnp.dot(rows, weight[...], preferred_element_type=F32)
    out[...] = total.astype(BF)


def hidden_kernel(parts_ref, out):
    blocks = parts_ref.shape[0]
    half = out.shape[2]
    total = parts_ref[0].astype(F32)
    for b in range(1, blocks):
        total = total + parts_ref[b].astype(F32)
    gate, up = total[:, :half], total[:, half:]
    hidden = (gate / (1.0 + jnp.exp(-gate)) * up).astype(BF)
    for b in range(blocks):
        out[b] = hidden


def down_kernel(lanes, hidden_ref, w0, w1, w2, w3, out, packed):
    count = out.shape[0]
    groups = count // 2
    width = w0.shape[0]
    span = 2 * width
    for k, weight in enumerate((w0, w1, w2, w3)):
        part = lax.dot_general(hidden_ref[...], weight[...], NT, preferred_element_type=F32)
        part = part.astype(BF)
        p, skip = k // 2, (k % 2) * width
        for i in range(lanes):
            at = i * span + skip
            piece = part[i * groups : (i + 1) * groups, :]
            packed[p * groups : (p + 1) * groups, at : at + width] = piece
    rows = lax.dot_general(halves_first(count), packed[...], TN, preferred_element_type=F32)
    out[...] = rows.astype(BF)


def mix_kernel(lanes, pick_ref, back_ref, high_ref, low_ref, out):
    _, width, tokens = out.shape
    span = 2 * width
    total = jnp.zeros((span, 2 * tokens), F32)
    for i in range(lanes):
        rows = back_ref[:, i * span : (i + 1) * span]
        total = total + lax.dot_general(rows, high_ref[i], TN, preferred_element_type=F32)
        total = total + lax.dot_general(rows, low_ref[i], TN, preferred_element_type=F32)
    place = pick_ref[2]
    for k in range(4):
        at, to = (k % 2) * width, (k // 2) * tokens
        out[place ^ (k ^ (k >> 1))] = total[at : at + width, to : to + tokens].astype(BF)


def join_kernel(parts_ref, out):
    total = parts_ref[0].astype(F32)
    for k in range(1, parts_ref.shape[0]):
        total = total + parts_ref[k].astype(F32)
    out[...] = total.astype(BF)


def latent_kernel(longest, lengths_ref, placement_ref, tokens_ref, weight_ref, out, select, offset):
    requests = lengths_ref.shape[1]
    rows = tokens_ref.shape[1]
    partial = lax.dot_general(tokens_ref[...], weight_ref[...], TN, preferred_element_type=F32)
    run = jnp.int32(0)
    for j in range(requests):
        offset[j] = run
        run = run + lengths_ref[0, j]
    place, position = iota((longest, rows), 0), iota((longest, rows), 1)
    for q in range(requests):
        request = placement_ref[0, q]
        hit = (position == place + offset[request]) & (place < lengths_ref[0, request])
        select[q * longest : (q + 1) * longest, :] = hit.astype(F32).astype(BF)
    picked = jnp.dot(select[...], partial.astype(BF), preferred_element_type=F32)
    out[...] = picked.astype(BF)


def norm_kernel(sum_ref, gain_ref, out):
    total = sum_ref[...]
    scale = lax.rsqrt(jnp.mean(total * total, axis=1, keepdims=True) + 1e-06)
    out[...] = (total * scale * gain_ref[...]).astype(BF)


def exchange(x, axes, groups=None):
    return lax.all_to_all(x, axes, split_axis=0, concat_axis=0, axis_index_groups=groups, tiled=True)


def flip(x, bits):
    return lax.ppermute(x, "dp", [(i, i ^ bits) for i in range(lax.axis_size("dp"))])


def gather_expert(array, resident):
    own = lax.dynamic_index_in_dim(array, resident, 0, keepdims=False)
    cross = lax.dynamic_index_in_dim(array, 1 - resident, 0, keepdims=False)
    second, third = flip(own, 1), flip(cross, 3)
    return own, second, third, flip(third, 1)


def sum_to_owner(parts):
    me = lax.axis_index("dp")
    bit = parts.shape[0] // 2
    while bit:
        high = (me & bit) != 0
        keep = jnp.where(high, parts[bit:], parts[:bit])
        send = jnp.where(high, parts[:bit], parts[bit:])
        parts = keep.astype(F32) + flip(send, bit).astype(F32)
        bit //= 2
        if bit:
            parts = parts.astype(BF)
    return parts[0]


def body(
    tokens, routes, route_weights, w_gate_up, w_down, w_latent, latent_gain, lengths, placement
):
    groups = lax.axis_size(SE)
    blocks = lax.axis_size("dp")
    along_y = 4
    spread = blocks // along_y
    near = [[along_y * x + y for y in range(along_y)] for x in range(spread)]
    far = [[along_y * x + y for x in range(spread)] for y in range(along_y)]
    rows, width = tokens.shape
    tops = routes.shape[1]
    residents = w_gate_up.shape[0]
    hidden_units = w_down.shape[1]
    latent_width = w_latent.shape[1]
    experts = residents * groups
    capacity = 5 * rows * tops // (4 * experts)
    lanes = capacity // 2
    longest = 2 * rows // blocks
    slots = 2 * groups
    row = 2 * lanes * width
    taken = lanes * groups
    share = taken // spread
    shape = jax.ShapeDtypeStruct
    tokens_t, routes_t, gates_t = tokens.T, routes.T, route_weights.T
    vmem = pl.BlockSpec(memory_space=pltpu.VMEM)
    smem = pl.BlockSpec(memory_space=pltpu.SMEM)

    at_y = lax.axis_index("dp") & (along_y - 1)
    resident = at_y >> 1
    pick = jnp.stack([resident, at_y & 1, at_y])

    with jax.named_scope("tokens"):
        flipped = [flip(tokens_t, bits) for bits in (2, 1, 3)]
        hot, own_tokens = call(
            functools.partial(hot_kernel, lanes),
            [shape((lanes, slots, 2 * rows), BF), shape((width, rows), BF)],
            pick,
            routes_t,
            tokens_t,
            in_specs=[smem, vmem, vmem],
            flops=2 * slots * rows * rows,
            moved=4 * lanes * slots * rows,
        )

    with jax.named_scope("dispatch"):
        outgoing = call(
            dispatch_kernel,
            shape((slots, row), BF),
            hot,
            own_tokens,
            flipped[1],
            flipped[2],
            flipped[0],
            flops=8 * slots * rows * width * lanes,
            moved=2 * slots * row,
        )
        outgoing, w_gate_up, w_down = lax.optimization_barrier((outgoing, w_gate_up, w_down))
        arrived = exchange(outgoing.reshape(groups, 2, row), SE)

    with jax.named_scope("gather"):
        up_blocks = gather_expert(w_gate_up, resident)
        down_blocks = gather_expert(w_down.transpose(0, 2, 1), resident)
        arrived, down_blocks = lax.optimization_barrier((arrived, down_blocks))

    with jax.named_scope("up"):
        columns = 2 * hidden_units
        step = 512 if columns % 512 == 0 else columns
        partial = pl.pallas_call(
            functools.partial(up_kernel, lanes),
            out_shape=shape((taken, columns), BF),
            grid=(columns // step,),
            in_specs=[pl.BlockSpec((slots, row), lambda c: (0, 0))]
            + [pl.BlockSpec((width, step), lambda c: (0, c))] * 4,
            out_specs=pl.BlockSpec((taken, step), lambda c: (0, c)),
            scratch_shapes=[pltpu.VMEM((taken, 4 * width), BF)],
            cost_estimate=pl.CostEstimate(
                flops=16 * taken * width * hidden_units,
                bytes_accessed=4 * hidden_units * (4 * width + taken),
                transcendentals=0,
            ),
            compiler_params=pltpu.CompilerParams(vmem_limit_bytes=24 * 1024 * 1024),
        )(arrived.reshape(slots, row), *up_blocks)
        shares = exchange(partial.reshape(spread, share, 2 * hidden_units), "dp", far)

    with jax.named_scope("hidden"):
        hidden = call(
            hidden_kernel,
            shape((spread, share, hidden_units), BF),
            shares,
            flops=2 * taken * hidden_units,
            moved=6 * taken * hidden_units,
        )
        gathered = exchange(hidden, "dp", far)

    with jax.named_scope("down"):
        produced = call(
            functools.partial(down_kernel, lanes),
            shape((slots, row), BF),
            gathered.reshape(taken, hidden_units),
            *down_blocks,
            scratch=[pltpu.VMEM((slots, row), BF)],
            flops=8 * taken * width * hidden_units,
            moved=2 * hidden_units * (4 * width + taken),
        )
        produced, tokens_t, gates_t = lax.optimization_barrier((produced, tokens_t, gates_t))
        back = exchange(produced.reshape(groups, 2, row), SE).reshape(slots, row)

    with jax.named_scope("gates"):
        gates = call(
            functools.partial(weights_kernel, lanes),
            [shape((lanes, slots, 2 * rows), BF)] * 2,
            pick,
            routes_t,
            gates_t,
            in_specs=[smem, vmem, vmem],
            flops=4 * slots * rows * rows,
            moved=8 * lanes * slots * rows,
        )

    with jax.named_scope("latent"):
        picked = call(
            functools.partial(latent_kernel, longest),
            shape((blocks * longest, latent_width), BF),
            lengths,
            placement,
            tokens_t,
            w_latent,
            in_specs=[smem, smem, vmem, vmem],
            scratch=[
                pltpu.VMEM((blocks * longest, rows), BF),
                pltpu.SMEM((blocks,), jnp.int32),
            ],
            flops=2 * rows * latent_width * (width + blocks * longest),
            moved=2 * latent_width * (width + blocks * longest),
        )
        latent = sum_to_owner(picked.reshape(blocks, longest, latent_width))
        latent_cache = call(
            norm_kernel,
            shape((longest, latent_width), BF),
            latent,
            latent_gain.reshape(1, latent_width),
            flops=8 * longest * latent_width,
            moved=4 * longest * latent_width,
        )
        back, latent_cache = lax.optimization_barrier((back, latent_cache))

    with jax.named_scope("mix"):
        parts = call(
            functools.partial(mix_kernel, lanes),
            shape((4, width, rows), BF),
            pick,
            back,
            *gates,
            in_specs=[smem] + [vmem] * 3,
            flops=32 * taken * width * rows,
            moved=2 * slots * row + 8 * lanes * slots * rows,
        )
        mixed = call(
            join_kernel,
            shape((width, rows), BF),
            exchange(parts, "dp", near),
            flops=3 * width * rows,
            moved=10 * width * rows,
        )
    return (mixed.T, latent_cache.reshape(1, 1, longest, latent_width))


def solution(mesh):
    return jax.shard_map(
        body,
        mesh=mesh,
        in_specs=(
            P(SE, "dp"),
            P(SE, None),
            P(SE, None),
            P(SE, "dp", None),
            P(SE, None, "dp"),
            P("dp", None),
            P(),
            P(SE, None),
            P(SE, None),
        ),
        out_specs=(P(SE, "dp"), P("dp", SE, None, None)),
        check_vma=False,
    )
```

```python
import functools

import jax
import jax.numpy as jnp
from jax import lax
from jax.experimental import pallas as pl
from jax.experimental.pallas import tpu as pltpu
from jax.sharding import PartitionSpec as P

SE = ("section", "expert")
NT = (((1,), (1,)), ((), ()))
TN = (((0,), (0,)), ((), ()))
BF = jnp.bfloat16
F32 = jnp.float32


def call(kernel, out_shape, *args, in_specs=None, scratch=(), flops=0, moved=0):
    kwargs = {}
    if in_specs is not None:
        kwargs["in_specs"] = in_specs
        kwargs["grid"] = (1,)
    return pl.pallas_call(
        kernel,
        out_shape=out_shape,
        scratch_shapes=list(scratch),
        cost_estimate=pl.CostEstimate(flops=flops, bytes_accessed=moved, transcendentals=0),
        compiler_params=pltpu.CompilerParams(vmem_limit_bytes=24 * 1024 * 1024),
        **kwargs,
    )(*args)


def iota(shape, dim):
    return lax.broadcasted_iota(jnp.int32, shape, dim)


def slot_masks(pick_ref, routes_t, lanes, groups):
    tops, rows = routes_t.shape
    resident, part = pick_ref[0], pick_ref[1]
    ids = iota((groups, rows), 0) * 2 + resident
    named = jnp.zeros((groups, rows), F32)
    for k in range(tops):
        named = named + jnp.where(routes_t[k : k + 1, :] == ids, 1.0, 0.0)
    earlier = (iota((rows, rows), 0) < iota((rows, rows), 1)).astype(F32).astype(BF)
    rank = jnp.dot(named.astype(BF), earlier, preferred_element_type=F32)
    base = (part * lanes).astype(F32)
    return ids, [(named > 0.5) & (rank == base + float(i)) for i in range(lanes)]


def hot_kernel(lanes, pick_ref, routes_ref, tokens_ref, out, tokens_out):
    groups = out.shape[0] // lanes
    _, masks = slot_masks(pick_ref, routes_ref[...], lanes, groups)
    for i, mask in enumerate(masks):
        out[i * groups : (i + 1) * groups, :] = mask.astype(F32).astype(BF)
    tokens_out[...] = tokens_ref[...]


def dispatch_kernel(hot_ref, t0, t1, t2, t3, out):
    _, groups, row = out.shape
    span = 2 * t0.shape[0]
    for p, (left, right) in enumerate(((t0, t1), (t2, t3))):
        both = jnp.concatenate([left[...], right[...]], axis=0)
        rows = lax.dot_general(hot_ref[...], both, NT, preferred_element_type=F32).astype(BF)
        for i in range(row // span):
            out[p, :, i * span : (i + 1) * span] = rows[i * groups : (i + 1) * groups, :]


def weights_kernel(lanes, pick_ref, routes_ref, weights_ref, out):
    routes_t, weights_t = routes_ref[...], weights_ref[...]
    groups, rows = out.shape[0] // lanes, routes_t.shape[1]
    ids, masks = slot_masks(pick_ref, routes_t, lanes, groups)
    gates = jnp.zeros(ids.shape, F32)
    for k in range(routes_t.shape[0]):
        gates = gates + jnp.where(routes_t[k : k + 1, :] == ids, weights_t[k : k + 1, :], 0.0)
    high = gates.astype(BF).astype(F32)
    low = gates - high
    for i, mask in enumerate(masks):
        out[i * groups : (i + 1) * groups, :rows] = jnp.where(mask, high, 0.0).astype(BF)
        out[i * groups : (i + 1) * groups, rows:] = jnp.where(mask, low, 0.0).astype(BF)


def up_kernel(rows_ref, w0, w1, w2, w3, out, packed):
    halves, groups, row = rows_ref.shape
    span = packed.shape[1] // halves

    @pl.when(pl.program_id(0) == 0)
    def _():
        for i in range(row // span):
            for p in range(halves):
                piece = rows_ref[p, :, i * span : (i + 1) * span]
                packed[i * groups : (i + 1) * groups, p * span : (p + 1) * span] = piece

    weight = jnp.concatenate([w0[...], w1[...], w2[...], w3[...]], axis=0)
    out[...] = jnp.dot(packed[...], weight, preferred_element_type=F32).astype(BF)


def hidden_kernel(parts_ref, out):
    blocks = parts_ref.shape[0]
    half = out.shape[2]
    total = parts_ref[0].astype(F32)
    for b in range(1, blocks):
        total = total + parts_ref[b].astype(F32)
    gate, up = total[:, :half], total[:, half:]
    hidden = (gate / (1.0 + jnp.exp(-gate)) * up).astype(BF)
    for b in range(blocks):
        out[b] = hidden


def down_kernel(hidden_ref, w0, w1, w2, w3, out):
    _, groups, row = out.shape
    span = 2 * w0.shape[0]
    for p, (left, right) in enumerate(((w0, w1), (w2, w3))):
        weight = jnp.concatenate([left[...], right[...]], axis=0)
        part = lax.dot_general(hidden_ref[...], weight, NT, preferred_element_type=F32).astype(BF)
        for i in range(row // span):
            out[p, :, i * span : (i + 1) * span] = part[i * groups : (i + 1) * groups, :]


def mix_kernel(pick_ref, back_ref, gates_ref, out):
    _, width, tokens = out.shape
    span = 2 * width
    place = pick_ref[2]
    for p in range(back_ref.shape[0]):
        pieces = [
            back_ref[p, :, at : at + span] for at in range(0, back_ref.shape[2], span)
        ]
        rows = jnp.concatenate(pieces, axis=0)
        total = lax.dot_general(rows, gates_ref[...], TN, preferred_element_type=F32)
        total = (total[:, :tokens] + total[:, tokens:]).astype(BF)
        for half in range(2):
            k = 2 * p + half
            out[place ^ (k ^ (k >> 1))] = total[half * width : (half + 1) * width, :]


def join_kernel(parts_ref, out):
    total = parts_ref[0].astype(F32)
    for k in range(1, parts_ref.shape[0]):
        total = total + parts_ref[k].astype(F32)
    out[...] = total.astype(BF)


def latent_kernel(longest, lengths_ref, placement_ref, tokens_ref, weight_ref, out, select, offset):
    requests = lengths_ref.shape[1]
    rows = tokens_ref.shape[1]
    partial = lax.dot_general(tokens_ref[...], weight_ref[...], TN, preferred_element_type=F32)
    run = jnp.int32(0)
    for j in range(requests):
        offset[j] = run
        run = run + lengths_ref[0, j]
    place, position = iota((longest, rows), 0), iota((longest, rows), 1)
    for q in range(requests):
        request = placement_ref[0, q]
        hit = (position == place + offset[request]) & (place < lengths_ref[0, request])
        select[q * longest : (q + 1) * longest, :] = hit.astype(F32).astype(BF)
    picked = jnp.dot(select[...], partial.astype(BF), preferred_element_type=F32)
    out[...] = picked.astype(BF)


def norm_kernel(sum_ref, gain_ref, out):
    total = sum_ref[...]
    scale = lax.rsqrt(jnp.mean(total * total, axis=1, keepdims=True) + 1e-06)
    out[...] = (total * scale * gain_ref[...]).astype(BF)


def exchange(x, axes, groups=None):
    return lax.all_to_all(x, axes, split_axis=0, concat_axis=0, axis_index_groups=groups, tiled=True)


def flip(x, bits):
    return lax.ppermute(x, "dp", [(i, i ^ bits) for i in range(lax.axis_size("dp"))])


def gather_expert(array, resident):
    own = lax.dynamic_index_in_dim(array, resident, 0, keepdims=False)
    cross = lax.dynamic_index_in_dim(array, 1 - resident, 0, keepdims=False)
    second, third = flip(own, 1), flip(cross, 3)
    return own, second, third, flip(third, 1)


def sum_to_owner(parts):
    me = lax.axis_index("dp")
    bit = parts.shape[0] // 2
    while bit:
        high = (me & bit) != 0
        keep = jnp.where(high, parts[bit:], parts[:bit])
        send = jnp.where(high, parts[:bit], parts[bit:])
        parts = keep.astype(F32) + flip(send, bit).astype(F32)
        bit //= 2
        if bit:
            parts = parts.astype(BF)
    return parts[0]


def body(
    tokens, routes, route_weights, w_gate_up, w_down, w_latent, latent_gain, lengths, placement
):
    groups = lax.axis_size(SE)
    blocks = lax.axis_size("dp")
    along_y = 4
    spread = blocks // along_y
    near = [[along_y * x + y for y in range(along_y)] for x in range(spread)]
    far = [[along_y * x + y for x in range(spread)] for y in range(along_y)]
    rows, width = tokens.shape
    tops = routes.shape[1]
    residents = w_gate_up.shape[0]
    hidden_units = w_down.shape[1]
    latent_width = w_latent.shape[1]
    experts = residents * groups
    capacity = 5 * rows * tops // (4 * experts)
    lanes = capacity // 2
    longest = 2 * rows // blocks
    slots = 2 * groups
    row = 2 * lanes * width
    taken = lanes * groups
    share = taken // spread
    shape = jax.ShapeDtypeStruct
    tokens_t, routes_t, gates_t = tokens.T, routes.T, route_weights.T
    vmem = pl.BlockSpec(memory_space=pltpu.VMEM)
    smem = pl.BlockSpec(memory_space=pltpu.SMEM)

    at_y = lax.axis_index("dp") & (along_y - 1)
    resident = at_y >> 1
    pick = jnp.stack([resident, at_y & 1, at_y])

    with jax.named_scope("tokens"):
        flipped = [flip(tokens_t, bits) for bits in (2, 1, 3)]
        hot, own_tokens = call(
            functools.partial(hot_kernel, lanes),
            [shape((taken, rows), BF), shape((width, rows), BF)],
            pick,
            routes_t,
            tokens_t,
            in_specs=[smem, vmem, vmem],
            flops=2 * slots * rows * rows,
            moved=4 * lanes * slots * rows,
        )

    with jax.named_scope("dispatch"):
        outgoing = call(
            dispatch_kernel,
            shape((2, groups, row), BF),
            hot,
            own_tokens,
            flipped[1],
            flipped[2],
            flipped[0],
            flops=8 * slots * rows * width * lanes,
            moved=2 * slots * row,
        )
        outgoing, w_gate_up, w_down = lax.optimization_barrier((outgoing, w_gate_up, w_down))
        arrived = exchange(outgoing.transpose(1, 0, 2), SE).transpose(1, 0, 2)

    with jax.named_scope("gather"):
        up_blocks = gather_expert(w_gate_up, resident)
        down_blocks = gather_expert(w_down.transpose(0, 2, 1), resident)
        arrived, down_blocks = lax.optimization_barrier((arrived, down_blocks))

    with jax.named_scope("up"):
        columns = 2 * hidden_units
        step = 512 if columns % 512 == 0 else columns
        partial = pl.pallas_call(
            up_kernel,
            out_shape=shape((taken, columns), BF),
            grid=(columns // step,),
            in_specs=[pl.BlockSpec((2, groups, row), lambda c: (0, 0, 0))]
            + [pl.BlockSpec((width, step), lambda c: (0, c))] * 4,
            out_specs=pl.BlockSpec((taken, step), lambda c: (0, c)),
            scratch_shapes=[pltpu.VMEM((taken, 4 * width), BF)],
            cost_estimate=pl.CostEstimate(
                flops=16 * taken * width * hidden_units,
                bytes_accessed=4 * hidden_units * (4 * width + taken),
                transcendentals=0,
            ),
            compiler_params=pltpu.CompilerParams(vmem_limit_bytes=24 * 1024 * 1024),
        )(arrived, *up_blocks)
        shares = exchange(partial.reshape(spread, share, 2 * hidden_units), "dp", far)

    with jax.named_scope("hidden"):
        hidden = call(
            hidden_kernel,
            shape((spread, share, hidden_units), BF),
            shares,
            flops=2 * taken * hidden_units,
            moved=6 * taken * hidden_units,
        )
        gathered = exchange(hidden, "dp", far)

    with jax.named_scope("down"):
        produced = call(
            down_kernel,
            shape((2, groups, row), BF),
            gathered.reshape(taken, hidden_units),
            *down_blocks,
            flops=8 * taken * width * hidden_units,
            moved=2 * hidden_units * (4 * width + taken),
        )
        produced, tokens_t, gates_t = lax.optimization_barrier((produced, tokens_t, gates_t))
        back = exchange(produced.transpose(1, 0, 2), SE).transpose(1, 0, 2)

    with jax.named_scope("gates"):
        gates = call(
            functools.partial(weights_kernel, lanes),
            shape((taken, 2 * rows), BF),
            pick,
            routes_t,
            gates_t,
            in_specs=[smem, vmem, vmem],
            flops=4 * slots * rows * rows,
            moved=8 * lanes * slots * rows,
        )

    with jax.named_scope("latent"):
        picked = call(
            functools.partial(latent_kernel, longest),
            shape((blocks * longest, latent_width), BF),
            lengths,
            placement,
            tokens_t,
            w_latent,
            in_specs=[smem, smem, vmem, vmem],
            scratch=[
                pltpu.VMEM((blocks * longest, rows), BF),
                pltpu.SMEM((blocks,), jnp.int32),
            ],
            flops=2 * rows * latent_width * (width + blocks * longest),
            moved=2 * latent_width * (width + blocks * longest),
        )
        latent = sum_to_owner(picked.reshape(blocks, longest, latent_width))
        latent_cache = call(
            norm_kernel,
            shape((longest, latent_width), BF),
            latent,
            latent_gain.reshape(1, latent_width),
            flops=8 * longest * latent_width,
            moved=4 * longest * latent_width,
        )
        back, latent_cache = lax.optimization_barrier((back, latent_cache))

    with jax.named_scope("mix"):
        parts = call(
            mix_kernel,
            shape((4, width, rows), BF),
            pick,
            back,
            gates,
            in_specs=[smem] + [vmem] * 2,
            flops=32 * taken * width * rows,
            moved=2 * slots * row + 8 * lanes * slots * rows,
        )
        mixed = call(
            join_kernel,
            shape((width, rows), BF),
            exchange(parts, "dp", near),
            flops=3 * width * rows,
            moved=10 * width * rows,
        )
    return (mixed.T, latent_cache.reshape(1, 1, longest, latent_width))


def solution(mesh):
    return jax.shard_map(
        body,
        mesh=mesh,
        in_specs=(
            P(SE, "dp"),
            P(SE, None),
            P(SE, None),
            P(SE, "dp", None),
            P(SE, None, "dp"),
            P("dp", None),
            P(),
            P(SE, None),
            P(SE, None),
        ),
        out_specs=(P(SE, "dp"), P("dp", SE, None, None)),
        check_vma=False,
    )
```

```python
import functools

import jax
import jax.numpy as jnp
from jax import lax
from jax.experimental import pallas as pl
from jax.experimental.pallas import tpu as pltpu
from jax.sharding import PartitionSpec as P

SE = ("section", "expert")
CHIPS = ("expert", "section")
NT = (((1,), (1,)), ((), ()))
TN = (((0,), (0,)), ((), ()))
BF = jnp.bfloat16
F32 = jnp.float32


def call(kernel, out_shape, *args, in_specs=None, scratch=(), flops=0, moved=0):
    kwargs = {}
    if in_specs is not None:
        kwargs["in_specs"] = in_specs
        kwargs["grid"] = (1,)
    return pl.pallas_call(
        kernel,
        out_shape=out_shape,
        scratch_shapes=list(scratch),
        cost_estimate=pl.CostEstimate(flops=flops, bytes_accessed=moved, transcendentals=0),
        compiler_params=pltpu.CompilerParams(vmem_limit_bytes=24 * 1024 * 1024),
        **kwargs,
    )(*args)


def iota(shape, dim):
    return lax.broadcasted_iota(jnp.int32, shape, dim)


def slot_masks(pick_ref, routes_t, lanes, groups):
    tops, rows = routes_t.shape
    resident, part = pick_ref[0], pick_ref[1]
    member = iota((groups, rows), 0)
    ids = ((member & 1) * (groups // 2) + (member >> 1)) * 2 + resident
    named = jnp.zeros((groups, rows), F32)
    for k in range(tops):
        named = named + jnp.where(routes_t[k : k + 1, :] == ids, 1.0, 0.0)
    earlier = (iota((rows, rows), 0) < iota((rows, rows), 1)).astype(F32).astype(BF)
    rank = jnp.dot(named.astype(BF), earlier, preferred_element_type=F32)
    base = (part * lanes).astype(F32)
    return ids, [(named > 0.5) & (rank == base + float(i)) for i in range(lanes)]


def hot_kernel(lanes, pick_ref, routes_ref, tokens_ref, out, tokens_out):
    groups = out.shape[0] // lanes
    _, masks = slot_masks(pick_ref, routes_ref[...], lanes, groups)
    for i, mask in enumerate(masks):
        out[i * groups : (i + 1) * groups, :] = mask.astype(F32).astype(BF)
    tokens_out[...] = tokens_ref[...]


def dispatch_kernel(hot_ref, t0, t1, t2, t3, out):
    _, groups, row = out.shape
    span = 2 * t0.shape[0]
    for p, (left, right) in enumerate(((t0, t1), (t2, t3))):
        both = jnp.concatenate([left[...], right[...]], axis=0)
        rows = lax.dot_general(hot_ref[...], both, NT, preferred_element_type=F32).astype(BF)
        for i in range(row // span):
            out[p, :, i * span : (i + 1) * span] = rows[i * groups : (i + 1) * groups, :]


def weights_kernel(lanes, pick_ref, routes_ref, weights_ref, out):
    routes_t, weights_t = routes_ref[...], weights_ref[...]
    groups, rows = out.shape[0] // lanes, routes_t.shape[1]
    ids, masks = slot_masks(pick_ref, routes_t, lanes, groups)
    gates = jnp.zeros(ids.shape, F32)
    for k in range(routes_t.shape[0]):
        gates = gates + jnp.where(routes_t[k : k + 1, :] == ids, weights_t[k : k + 1, :], 0.0)
    high = gates.astype(BF).astype(F32)
    low = gates - high
    for i, mask in enumerate(masks):
        out[i * groups : (i + 1) * groups, :rows] = jnp.where(mask, high, 0.0).astype(BF)
        out[i * groups : (i + 1) * groups, rows:] = jnp.where(mask, low, 0.0).astype(BF)


def up_kernel(rows_ref, w0, w1, w2, w3, out, packed):
    halves, groups, row = rows_ref.shape
    span = packed.shape[1] // halves

    @pl.when(pl.program_id(0) == 0)
    def _():
        for i in range(row // span):
            for p in range(halves):
                piece = rows_ref[p, :, i * span : (i + 1) * span]
                packed[i * groups : (i + 1) * groups, p * span : (p + 1) * span] = piece

    weight = jnp.concatenate([w0[...], w1[...], w2[...], w3[...]], axis=0)
    out[...] = jnp.dot(packed[...], weight, preferred_element_type=F32).astype(BF)


def hidden_kernel(parts_ref, out):
    blocks = parts_ref.shape[0]
    half = out.shape[2]
    total = parts_ref[0].astype(F32)
    for b in range(1, blocks):
        total = total + parts_ref[b].astype(F32)
    gate, up = total[:, :half], total[:, half:]
    hidden = (gate / (1.0 + jnp.exp(-gate)) * up).astype(BF)
    for b in range(blocks):
        out[b] = hidden


def halves_first(count):
    a = iota((count, count), 1)
    return (iota((count, count), 0) == (a & 1) * (count // 2) + (a >> 1)).astype(F32).astype(BF)


def down_kernel(lanes, hidden_ref, w0, w1, w2, w3, out, packed):
    count = out.shape[0]
    groups = count // 2
    width = w0.shape[0]
    span = 2 * width
    for k, weight in enumerate((w0, w1, w2, w3)):
        part = lax.dot_general(hidden_ref[...], weight[...], NT, preferred_element_type=F32)
        part = part.astype(BF)
        p, skip = k // 2, (k % 2) * width
        for i in range(lanes):
            at = i * span + skip
            piece = part[i * groups : (i + 1) * groups, :]
            packed[p * groups : (p + 1) * groups, at : at + width] = piece
    rows = lax.dot_general(halves_first(count), packed[...], TN, preferred_element_type=F32)
    out[...] = rows.astype(BF)


def mix_kernel(pick_ref, back_ref, gates_ref, out):
    _, width, tokens = out.shape
    span = 2 * width
    place = pick_ref[2]
    for p in range(back_ref.shape[0]):
        pieces = [
            back_ref[p, :, at : at + span] for at in range(0, back_ref.shape[2], span)
        ]
        rows = jnp.concatenate(pieces, axis=0)
        total = lax.dot_general(rows, gates_ref[...], TN, preferred_element_type=F32)
        total = (total[:, :tokens] + total[:, tokens:]).astype(BF)
        for half in range(2):
            k = 2 * p + half
            out[place ^ (k ^ (k >> 1))] = total[half * width : (half + 1) * width, :]


def join_kernel(parts_ref, out):
    total = parts_ref[0].astype(F32)
    for k in range(1, parts_ref.shape[0]):
        total = total + parts_ref[k].astype(F32)
    out[...] = total.astype(BF)


def latent_kernel(longest, lengths_ref, placement_ref, tokens_ref, weight_ref, out, select, offset):
    requests = lengths_ref.shape[1]
    rows = tokens_ref.shape[1]
    partial = lax.dot_general(tokens_ref[...], weight_ref[...], TN, preferred_element_type=F32)
    run = jnp.int32(0)
    for j in range(requests):
        offset[j] = run
        run = run + lengths_ref[0, j]
    place, position = iota((longest, rows), 0), iota((longest, rows), 1)
    for q in range(requests):
        request = placement_ref[0, q]
        hit = (position == place + offset[request]) & (place < lengths_ref[0, request])
        select[q * longest : (q + 1) * longest, :] = hit.astype(F32).astype(BF)
    picked = jnp.dot(select[...], partial.astype(BF), preferred_element_type=F32)
    out[...] = picked.astype(BF)


def norm_kernel(sum_ref, gain_ref, out):
    total = sum_ref[...]
    scale = lax.rsqrt(jnp.mean(total * total, axis=1, keepdims=True) + 1e-06)
    out[...] = (total * scale * gain_ref[...]).astype(BF)


def exchange(x, axes, groups=None):
    return lax.all_to_all(x, axes, split_axis=0, concat_axis=0, axis_index_groups=groups, tiled=True)


def flip(x, bits):
    return lax.ppermute(x, "dp", [(i, i ^ bits) for i in range(lax.axis_size("dp"))])


def gather_expert(array, resident):
    own = lax.dynamic_index_in_dim(array, resident, 0, keepdims=False)
    cross = lax.dynamic_index_in_dim(array, 1 - resident, 0, keepdims=False)
    second, third = flip(own, 1), flip(cross, 3)
    return own, second, third, flip(third, 1)


def sum_to_owner(parts):
    me = lax.axis_index("dp")
    bit = parts.shape[0] // 2
    while bit:
        high = (me & bit) != 0
        keep = jnp.where(high, parts[bit:], parts[:bit])
        send = jnp.where(high, parts[:bit], parts[bit:])
        parts = keep.astype(F32) + flip(send, bit).astype(F32)
        bit //= 2
        if bit:
            parts = parts.astype(BF)
    return parts[0]


def body(
    tokens, routes, route_weights, w_gate_up, w_down, w_latent, latent_gain, lengths, placement
):
    groups = lax.axis_size(SE)
    blocks = lax.axis_size("dp")
    along_y = 4
    spread = blocks // along_y
    near = [[along_y * x + y for y in range(along_y)] for x in range(spread)]
    far = [[along_y * x + y for x in range(spread)] for y in range(along_y)]
    rows, width = tokens.shape
    tops = routes.shape[1]
    residents = w_gate_up.shape[0]
    hidden_units = w_down.shape[1]
    latent_width = w_latent.shape[1]
    experts = residents * groups
    capacity = 5 * rows * tops // (4 * experts)
    lanes = capacity // 2
    longest = 2 * rows // blocks
    slots = 2 * groups
    row = 2 * lanes * width
    taken = lanes * groups
    share = taken // spread
    shape = jax.ShapeDtypeStruct
    tokens_t, routes_t, gates_t = tokens.T, routes.T, route_weights.T
    vmem = pl.BlockSpec(memory_space=pltpu.VMEM)
    smem = pl.BlockSpec(memory_space=pltpu.SMEM)

    at_y = lax.axis_index("dp") & (along_y - 1)
    resident = at_y >> 1
    pick = jnp.stack([resident, at_y & 1, at_y])

    with jax.named_scope("tokens"):
        flipped = [flip(tokens_t, bits) for bits in (2, 1, 3)]
        hot, own_tokens = call(
            functools.partial(hot_kernel, lanes),
            [shape((taken, rows), BF), shape((width, rows), BF)],
            pick,
            routes_t,
            tokens_t,
            in_specs=[smem, vmem, vmem],
            flops=2 * slots * rows * rows,
            moved=4 * lanes * slots * rows,
        )

    with jax.named_scope("dispatch"):
        outgoing = call(
            dispatch_kernel,
            shape((2, groups, row), BF),
            hot,
            own_tokens,
            flipped[1],
            flipped[2],
            flipped[0],
            flops=8 * slots * rows * width * lanes,
            moved=2 * slots * row,
        )
        outgoing, w_gate_up, w_down = lax.optimization_barrier((outgoing, w_gate_up, w_down))
        arrived = exchange(outgoing.transpose(1, 0, 2), CHIPS).transpose(1, 0, 2)

    with jax.named_scope("gather"):
        up_blocks = gather_expert(w_gate_up, resident)
        down_blocks = gather_expert(w_down.transpose(0, 2, 1), resident)
        arrived, down_blocks = lax.optimization_barrier((arrived, down_blocks))

    with jax.named_scope("up"):
        columns = 2 * hidden_units
        step = 512 if columns % 512 == 0 else columns
        partial = pl.pallas_call(
            up_kernel,
            out_shape=shape((taken, columns), BF),
            grid=(columns // step,),
            in_specs=[pl.BlockSpec((2, groups, row), lambda c: (0, 0, 0))]
            + [pl.BlockSpec((width, step), lambda c: (0, c))] * 4,
            out_specs=pl.BlockSpec((taken, step), lambda c: (0, c)),
            scratch_shapes=[pltpu.VMEM((taken, 4 * width), BF)],
            cost_estimate=pl.CostEstimate(
                flops=16 * taken * width * hidden_units,
                bytes_accessed=4 * hidden_units * (4 * width + taken),
                transcendentals=0,
            ),
            compiler_params=pltpu.CompilerParams(vmem_limit_bytes=24 * 1024 * 1024),
        )(arrived, *up_blocks)
        shares = exchange(partial.reshape(spread, share, 2 * hidden_units), "dp", far)

    with jax.named_scope("hidden"):
        hidden = call(
            hidden_kernel,
            shape((spread, share, hidden_units), BF),
            shares,
            flops=2 * taken * hidden_units,
            moved=6 * taken * hidden_units,
        )
        gathered = exchange(hidden, "dp", far)

    with jax.named_scope("down"):
        produced = call(
            functools.partial(down_kernel, lanes),
            shape((slots, row), BF),
            gathered.reshape(taken, hidden_units),
            *down_blocks,
            scratch=[pltpu.VMEM((slots, row), BF)],
            flops=8 * taken * width * hidden_units,
            moved=2 * hidden_units * (4 * width + taken),
        )
        produced, tokens_t, gates_t = lax.optimization_barrier((produced, tokens_t, gates_t))
        back = exchange(produced.reshape(groups, 2, row), CHIPS).transpose(1, 0, 2)

    with jax.named_scope("gates"):
        gates = call(
            functools.partial(weights_kernel, lanes),
            shape((taken, 2 * rows), BF),
            pick,
            routes_t,
            gates_t,
            in_specs=[smem, vmem, vmem],
            flops=4 * slots * rows * rows,
            moved=8 * lanes * slots * rows,
        )

    with jax.named_scope("latent"):
        picked = call(
            functools.partial(latent_kernel, longest),
            shape((blocks * longest, latent_width), BF),
            lengths,
            placement,
            tokens_t,
            w_latent,
            in_specs=[smem, smem, vmem, vmem],
            scratch=[
                pltpu.VMEM((blocks * longest, rows), BF),
                pltpu.SMEM((blocks,), jnp.int32),
            ],
            flops=2 * rows * latent_width * (width + blocks * longest),
            moved=2 * latent_width * (width + blocks * longest),
        )
        latent = sum_to_owner(picked.reshape(blocks, longest, latent_width))
        latent_cache = call(
            norm_kernel,
            shape((longest, latent_width), BF),
            latent,
            latent_gain.reshape(1, latent_width),
            flops=8 * longest * latent_width,
            moved=4 * longest * latent_width,
        )
        back, latent_cache = lax.optimization_barrier((back, latent_cache))

    with jax.named_scope("mix"):
        parts = call(
            mix_kernel,
            shape((4, width, rows), BF),
            pick,
            back,
            gates,
            in_specs=[smem] + [vmem] * 2,
            flops=32 * taken * width * rows,
            moved=2 * slots * row + 8 * lanes * slots * rows,
        )
        mixed = call(
            join_kernel,
            shape((width, rows), BF),
            exchange(parts, "dp", near),
            flops=3 * width * rows,
            moved=10 * width * rows,
        )
    return (mixed.T, latent_cache.reshape(1, 1, longest, latent_width))


def solution(mesh):
    return jax.shard_map(
        body,
        mesh=mesh,
        in_specs=(
            P(SE, "dp"),
            P(SE, None),
            P(SE, None),
            P(SE, "dp", None),
            P(SE, None, "dp"),
            P("dp", None),
            P(),
            P(SE, None),
            P(SE, None),
        ),
        out_specs=(P(SE, "dp"), P("dp", SE, None, None)),
        check_vma=False,
    )
```
